256 devices in a mesh: rows: 256 (over y, x, z, core).
Axes of the slice: x: 4, y: 4, z: 8, core: 2. Of those that a mesh axis runs over, the one named last changes fastest.
Arguments:
- query: bfloat16 [65536, 2048], P('rows'), may hold values from -114 to 114
- response_keys: bfloat16 [65536, 256], P('rows'), may hold values from -6 to 6
- response_values: bfloat16 [65536, 256], P('rows'), may hold values from -6 to 6
- prompt_keys: bfloat16 [32768, 256], P('rows'), may hold values from -6.1 to 6.1
- prompt_values: bfloat16 [32768, 256], P('rows'), may hold values from -6 to 6
- dout: bfloat16 [65536, 2048], P('rows'), may hold values from -6 to 6
- row_slot: int32 [65536], P('rows'), may hold values from -1 to 3, as said below
- row_pos: int32 [65536], P('rows'), may hold values from 0 to 255, as said below
Outputs:
- attended_out: bfloat16 [65536, 2048], P('rows')
- grad_query: bfloat16 [65536, 2048], P('rows')
- grad_response_keys: bfloat16 [65536, 256], P('rows')
- grad_response_values: bfloat16 [65536, 256], P('rows')
- grad_prompt_keys: bfloat16 [32768, 256], P('rows')
- grad_prompt_values: bfloat16 [32768, 256], P('rows')
The draws below stay inside these ranges and needn't reach their ends.
Inputs may be any that keep to these rules, and one draw needn't show every extreme that they name: `row_slot`: every response of a prompt lies whole, in consecutive rows and positions 0, 1, 2 and so on, on one device of that prompt's 4 devices; a prompt has 4 responses of 64 to 256 rows each, and in every group some device is filled by one response of 256 rows. Other rows are empty. `row_pos`: 0 on empty rows.
All inputs are finite; a program needn't handle non-finite values.
Results may differ from the reference program's by a relative error of at most 0.0065.
Values may be sent and summed in bfloat16 or wider, within the bound.
No kernel may reach another device: no remote copies, remote signals or barrier semaphores. Data moves between devices by JAX's collectives and lax.ppermute only.
A program may use at most 128 MiB of HBM per device.

```python
import jax
import jax.numpy as jnp
from jax import lax

QUERY_HEADS = 16
KV_HEADS = 2
HEAD_DIM = 128
RESP_DEV = 256
PROMPT_DEV = 128
GROUP = 4
NRESP = 4
PLEN = 512
PROMPTS = 64
PROMPT_TOKENS = 32768
RESP_TOKENS = 65536
N_ROWS = 256


def packed_rows(key):
    key = jax.random.fold_in(key, 501)
    lengths = jax.random.randint(jax.random.fold_in(key, 1), (PROMPTS, NRESP), RESP_DEV // 4, RESP_DEV + 1)
    forced = jax.random.randint(jax.random.fold_in(key, 2), (PROMPTS, 1), 0, NRESP)
    lengths = jnp.where(jnp.arange(NRESP)[None, :] == forced, RESP_DEV, lengths).astype(jnp.int32)
    filled = jnp.zeros((PROMPTS, GROUP), jnp.int32)
    members = jnp.arange(GROUP, dtype=jnp.int32)[None, :]
    targets = []
    starts = []
    for response in range(NRESP):
        length = lengths[:, response:response + 1]
        fitting = (filled + length <= RESP_DEV).astype(jnp.int32)
        target = jnp.argmax(fitting, axis=1).astype(jnp.int32)[:, None]
        chosen = members == target
        starts.append(jnp.sum(jnp.where(chosen, filled, 0), axis=1))
        targets.append(target[:, 0])
        filled = filled + jnp.where(chosen, length, 0)
    target_all = jnp.stack(targets, axis=1)
    start_all = jnp.stack(starts, axis=1)
    cells = jnp.arange(RESP_DEV, dtype=jnp.int32)[None, None, :, None]
    inside = target_all[:, None, None, :] == members[0][None, :, None, None]
    inside = inside & (start_all[:, None, None, :] <= cells) & (cells < (start_all + lengths)[:, None, None, :])
    slot_ids = jnp.arange(NRESP, dtype=jnp.int32)[None, None, None, :] + 1
    slots = jnp.sum(jnp.where(inside, slot_ids, 0), axis=-1) - 1
    offsets = jnp.sum(jnp.where(inside, cells - start_all[:, None, None, :], 0), axis=-1)
    slots = slots.transpose(1, 0, 2)
    offsets = offsets.transpose(1, 0, 2)
    return (slots.reshape(-1).astype(jnp.int32), offsets.reshape(-1).astype(jnp.int32))


def prompt_base(key):
    base = jax.random.normal(jax.random.fold_in(key, 707), (PROMPT_TOKENS, KV_HEADS * HEAD_DIM), jnp.float32)
    return jnp.clip(base, -6.0, 6.0)


def draw_row_slot(key, part):
    slots, offsets = packed_rows(key)
    return slots


def draw_row_pos(key, part):
    slots, offsets = packed_rows(key)
    return offsets


def draw_prompt_keys(key, part):
    base = prompt_base(key)
    return base.astype(jnp.bfloat16)


def draw_query(key, part):
    key = jax.random.fold_in(key, 5)
    fresh = jnp.clip(jax.random.normal(key, (RESP_TOKENS, QUERY_HEADS * HEAD_DIM), jnp.float32), -6.0, 6.0)
    return fresh.astype(jnp.bfloat16)


def shard_levels(own_key, shape, shards, low, largest):
    factor_of, own = 1.0, jax.random.fold_in(own_key, 6)
    for position, blocks in shards:
        draws = jnp.exp(jax.random.uniform(jax.random.fold_in(own, position), (blocks,), jnp.float32, low / len(shards), largest / len(shards)))
        factor_of = factor_of * jnp.repeat(draws, shape[position] // blocks).reshape([-1 if axis == position else 1 for axis in range(len(shape))])
    return factor_of


def gaussian(key, shape, spread, bound, split=(), kind=jnp.bfloat16):
    entries = spread * jax.random.normal(key, shape, jnp.float32)
    if split:
        entries = entries * shard_levels(key, shape, split, -0.22, 0.18)
    return jnp.clip(entries, -bound, bound).astype(kind)


def setup_inputs(seed: int = 0) -> dict:
    keys = jax.random.split(jax.random.key(seed), 9)
    return {
        "query": draw_query(jax.random.fold_in(keys[8], 71), 0),
        "response_keys": gaussian(keys[1], (RESP_TOKENS, KV_HEADS * HEAD_DIM), 1.0, 6.0, ((0, 256),)),
        "response_values": gaussian(keys[2], (RESP_TOKENS, KV_HEADS * HEAD_DIM), 1.0, 6.0, ((0, 256),)),
        "prompt_keys": draw_prompt_keys(jax.random.fold_in(keys[8], 71), 0),
        "prompt_values": gaussian(keys[4], (PROMPT_TOKENS, KV_HEADS * HEAD_DIM), 1.0, 6.0, ((0, 256),)),
        "dout": gaussian(keys[5], (RESP_TOKENS, QUERY_HEADS * HEAD_DIM), 1.0, 6.0, ((0, 256),)),
        "row_slot": draw_row_slot(jax.random.fold_in(keys[8], 71), 0),
        "row_pos": draw_row_pos(jax.random.fold_in(keys[8], 71), 0),
    }


def head_pass(query_rows, grad_rows, key_rows, value_rows, allowed, group_heads):
    row_count = allowed.shape[0]
    scores = jnp.dot(query_rows, key_rows.T, preferred_element_type=jnp.float32) * (HEAD_DIM ** -0.5)
    scores = scores.reshape(row_count, group_heads, -1)
    scores = jnp.where(allowed[:, None, :], scores, jnp.float32(-1e30))
    scores = scores.reshape(row_count * group_heads, -1)
    biggest = jnp.max(scores, axis=1, keepdims=True)
    weights = jnp.exp(scores - biggest)
    weights = weights / jnp.sum(weights, axis=1, keepdims=True)
    weights_low = weights.astype(jnp.bfloat16)
    attended = jnp.dot(weights_low, value_rows, preferred_element_type=jnp.float32)
    pressure = jnp.dot(grad_rows, value_rows.T, preferred_element_type=jnp.float32)
    centre = jnp.sum(weights * pressure, axis=1, keepdims=True)
    slopes = (weights * (pressure - centre) * (HEAD_DIM ** -0.5)).astype(jnp.bfloat16)
    grad_q = jnp.dot(slopes, key_rows, preferred_element_type=jnp.float32)
    grad_k = jnp.dot(slopes.T, query_rows, preferred_element_type=jnp.float32)
    grad_v = jnp.dot(weights_low.T, grad_rows, preferred_element_type=jnp.float32)
    return attended, grad_q, grad_k, grad_v


def device_block(query, response_keys, response_values, prompt_keys, prompt_values, dout, row_slot, row_pos):
    row_count = query.shape[0]
    prompt_rows = prompt_keys.shape[0]
    live_rows = row_slot >= 0
    same_resp = (row_slot[:, None] == row_slot[None, :]) & live_rows[None, :] & (row_pos[None, :] <= row_pos[:, None])
    allowed = jnp.concatenate([jnp.ones((row_count, prompt_rows), dtype=bool), same_resp], axis=1)
    grad_live = jnp.where(live_rows[:, None], dout, jnp.zeros_like(dout))
    all_keys = jnp.concatenate([prompt_keys, response_keys], axis=0)
    all_values = jnp.concatenate([prompt_values, response_values], axis=0)
    group_heads = QUERY_HEADS // KV_HEADS
    width_cols = group_heads * HEAD_DIM
    outs_list, dq_list, dk_list, dv_list = [], [], [], []
    for kv_head in range(KV_HEADS):
        query_cols = query[:, kv_head * width_cols:(kv_head + 1) * width_cols].reshape(row_count * group_heads, HEAD_DIM)
        grad_cols = grad_live[:, kv_head * width_cols:(kv_head + 1) * width_cols].reshape(row_count * group_heads, HEAD_DIM)
        key_cols = all_keys[:, kv_head * HEAD_DIM:(kv_head + 1) * HEAD_DIM]
        value_cols = all_values[:, kv_head * HEAD_DIM:(kv_head + 1) * HEAD_DIM]
        attended, grad_q, grad_k, grad_v = head_pass(query_cols, grad_cols, key_cols, value_cols, allowed, group_heads)
        outs_list.append(attended.reshape(row_count, width_cols))
        dq_list.append(grad_q.reshape(row_count, width_cols))
        dk_list.append(grad_k)
        dv_list.append(grad_v)
    outputs = jnp.concatenate(outs_list, axis=1)
    outputs = jnp.where(live_rows[:, None], outputs, jnp.zeros_like(outputs)).astype(jnp.bfloat16)
    grad_query = jnp.concatenate(dq_list, axis=1).astype(jnp.bfloat16)
    key_terms = jnp.concatenate(dk_list, axis=1)
    value_terms = jnp.concatenate(dv_list, axis=1)
    return (outputs, grad_query, key_terms[prompt_rows:].astype(jnp.bfloat16), value_terms[prompt_rows:].astype(jnp.bfloat16),
            key_terms[:prompt_rows].astype(jnp.bfloat16), value_terms[:prompt_rows].astype(jnp.bfloat16))


def reference(query, response_keys, response_values, prompt_keys, prompt_values, dout, row_slot, row_pos):
    width = KV_HEADS * HEAD_DIM
    key_view = prompt_keys.reshape(GROUP, PROMPTS, PROMPT_DEV, width)
    value_view = prompt_values.reshape(GROUP, PROMPTS, PROMPT_DEV, width)

    def one_device(index):
        first = (index * RESP_DEV).astype(jnp.int32)
        prompt_index = (index % PROMPTS).astype(jnp.int32)

        def rows_of(array):
            return lax.dynamic_slice_in_dim(array, first, RESP_DEV, 0)

        def prompt_of(view):
            return lax.dynamic_index_in_dim(view, prompt_index, 1, keepdims=False).reshape(PLEN, width)

        return device_block(rows_of(query), rows_of(response_keys), rows_of(response_values), prompt_of(key_view),
                            prompt_of(value_view), rows_of(dout), rows_of(row_slot), rows_of(row_pos))

    results = lax.map(one_device, jnp.arange(N_ROWS, dtype=jnp.int32))
    attended_out = results[0].reshape(RESP_TOKENS, QUERY_HEADS * HEAD_DIM)
    grad_query = results[1].reshape(RESP_TOKENS, QUERY_HEADS * HEAD_DIM)
    grad_response_keys = results[2].reshape(RESP_TOKENS, width)
    grad_response_values = results[3].reshape(RESP_TOKENS, width)

    def back_to_layout(parts):
        summed = jnp.sum(parts.astype(jnp.float32).reshape(GROUP, PROMPTS, PLEN, width), axis=0)
        summed = summed.reshape(PROMPTS, GROUP, PROMPT_DEV, width).transpose(1, 0, 2, 3)
        return summed.reshape(PROMPT_TOKENS, width).astype(jnp.bfloat16)

    grad_prompt_keys = back_to_layout(results[4])
    grad_prompt_values = back_to_layout(results[5])
    return (attended_out, grad_query, grad_response_keys, grad_response_values, grad_prompt_keys, grad_prompt_values)
```

```python
import jax
import jax.numpy as jnp
from jax import lax
from jax.experimental import pallas as pl
from jax.experimental.pallas import tpu as pltpu
from jax.sharding import PartitionSpec as P

QUERY_HEADS = 16
KV_HEADS = 2
GROUP_HEADS = QUERY_HEADS // KV_HEADS
HEAD_DIM = 128
GROUP = 4
ROWS = 256
HALF = 128
SHARD = 128
REMOTE = (GROUP - 1) * SHARD
SCALE = HEAD_DIM**-0.5
EXP2_SCALE = SCALE * 1.4426950408889634
NEG = -1e30
F32 = jnp.float32
BF16 = jnp.bfloat16
VM = pltpu.VMEM


def dot_nt(a, b):
    return lax.dot_general(a, b, (((1,), (1,)), ((), ())), preferred_element_type=F32)


def dot_nn(a, b):
    return lax.dot_general(a, b, (((1,), (0,)), ((), ())), preferred_element_type=F32)


def col_max(x):
    return jnp.max(x, axis=0, keepdims=True)


def col_sum(x):
    return jnp.sum(x, axis=0, keepdims=True)


def second_half(a, b):
    return jnp.concatenate([a[HALF:], b[HALF:]], axis=0)


def halves(a, b):
    return jnp.concatenate([a[:, HALF:], b[:, HALF:]], axis=1)


def unhalves(x, which, fill):
    return jnp.concatenate([fill, x[:, which * HALF : (which + 1) * HALF]], axis=1)


def local_forward(
    q_in, do_in, pk, pv, rk, rv, slot_in, pos_in,
    q, do, kv, p1, dp1, p2, dp2, m_out, l_out, c_out, live,
    bias, slot, pos, sems,
):
    width = GROUP_HEADS * HEAD_DIM
    pieces = [
        (slot_in, slot),
        (pos_in, pos),
        (pk, kv.at[0, pl.ds(0, SHARD)]),
        (rk, kv.at[0, pl.ds(SHARD, ROWS)]),
        (pv, kv.at[1, pl.ds(0, SHARD)]),
        (rv, kv.at[1, pl.ds(SHARD, ROWS)]),
    ]
    for g in range(KV_HEADS):
        span = pl.ds(g * width, width)
        pieces.append((q_in.at[:, span], q.at[:, span]))
        pieces.append((do_in.at[:, span], do.at[:, span]))
    copies = [pltpu.make_async_copy(a, b, sems.at[n]) for n, (a, b) in enumerate(pieces)]
    for copy in copies:
        copy.start()
    copies[0].wait()
    copies[1].wait()
    slot_row = jnp.broadcast_to(slot[...], (ROWS, ROWS)).astype(F32)
    pos_row = jnp.broadcast_to(pos[...], (ROWS, ROWS)).astype(F32)
    slot_col = slot_row.T
    pos_col = pos_row.T
    seen = (slot_col == slot_row) & (slot_col >= 0) & (pos_col <= pos_row)
    bias[...] = jnp.where(seen, 0.0, NEG)
    live[...] = (slot[...] >= 0).astype(F32)
    nothing = jnp.full((1, HALF), NEG, F32)
    zero = jnp.zeros((1, HALF), F32)
    near = SHARD + HALF
    for copy in copies[2:6]:
        copy.wait()
    for g in range(KV_HEADS):
        copies[6 + 2 * g].wait()
        copies[7 + 2 * g].wait()
        cols = slice(g * HEAD_DIM, (g + 1) * HEAD_DIM)
        k1 = kv[0, :near, cols]
        v1 = kv[1, :near, cols]
        k2 = kv[0, near:, cols]
        v2 = kv[1, near:, cols]
        for pair in range(GROUP_HEADS // 2):
            first = g * GROUP_HEADS + 2 * pair
            qs = [q[:, h * HEAD_DIM : (h + 1) * HEAD_DIM] for h in (first, first + 1)]
            ds = [do[:, h * HEAD_DIM : (h + 1) * HEAD_DIM] for h in (first, first + 1)]
            b2 = bias[HALF:, HALF:]
            s2 = dot_nt(k2, second_half(*qs)) + jnp.concatenate([b2, b2], axis=1)
            m2 = col_max(s2)
            ms, ls, cs = [], [], []
            for i in range(2):
                s1 = dot_nt(k1, qs[i])
                s1 = jnp.concatenate([s1[:SHARD], s1[SHARD:] + bias[:HALF, :]], axis=0)
                m = jnp.maximum(col_max(s1), unhalves(m2, i, nothing))
                e1 = jnp.exp2((s1 - m) * EXP2_SCALE)
                g1 = dot_nt(v1, ds[i])
                p1[first + i] = e1
                dp1[first + i] = g1
                ms.append(m)
                ls.append(col_sum(e1))
                cs.append(col_sum(e1 * g1))
            e2 = jnp.exp2((s2 - halves(*ms)) * EXP2_SCALE)
            g2 = dot_nt(v2, second_half(*ds))
            p2[first // 2] = e2
            dp2[first // 2] = g2
            l2 = col_sum(e2)
            c2 = col_sum(e2 * g2)
            for i in range(2):
                h = first + i
                m_out[h : h + 1, :] = ms[i]
                l_out[h : h + 1, :] = ls[i] + unhalves(l2, i, zero)
                c_out[h : h + 1, :] = cs[i] + unhalves(c2, i, zero)


def remote_pass(
    q, do, r1, r2, r3, live, m_in, l_in, c_in, w_out, ds_out, f_out, d_out, g1, g2, g3
):
    shards = (r1, r2, r3)
    outs = (g1, g2, g3)
    alive = live[...]
    blocks = [slice(n * SHARD, (n + 1) * SHARD) for n in range(GROUP - 1)]
    columns = [slice(g * HEAD_DIM, (g + 1) * HEAD_DIM) for g in range(KV_HEADS)]
    keys = [jnp.concatenate([r[0, :, c] for r in shards], axis=0) for c in columns]
    values = [jnp.concatenate([r[1, :, c] for r in shards], axis=0) for c in columns]

    def head(ref, h):
        return ref[:, h * HEAD_DIM : (h + 1) * HEAD_DIM]

    def slopes_of(h):
        g = h // GROUP_HEADS
        s = dot_nt(keys[g], head(q, h))
        pressure = dot_nt(values[g], head(do, h))
        m_old = m_in[h : h + 1, :]
        tops = [col_max(s[b]) for b in blocks]
        es = [jnp.exp2((s[b] - top) * EXP2_SCALE) for b, top in zip(blocks, tops)]
        m = m_old
        for top in tops:
            m = jnp.maximum(m, top)
        back = jnp.exp2((m_old - m) * EXP2_SCALE)
        total = l_in[h : h + 1, :] * back
        centre = c_in[h : h + 1, :] * back
        factors = []
        for b, top, e in zip(blocks, tops, es):
            factor = jnp.exp2((top - m) * EXP2_SCALE)
            total = total + col_sum(e) * factor
            centre = centre + col_sum(e * pressure[b]) * factor
            factors.append(factor)
        inv = 1.0 / total
        centre = centre * inv
        inv = inv * alive
        f_out[h : h + 1, :] = back * inv
        d_out[h : h + 1, :] = centre
        lows, slopes = [], []
        for b, e, factor in zip(blocks, es, factors):
            w = e * (factor * inv)
            lows.append(w.astype(BF16))
            slopes.append((w * (pressure[b] - centre)).astype(BF16))
            w_out[h, b] = lows[-1]
            ds_out[h, b] = slopes[-1]
        return jnp.concatenate(lows, axis=0), jnp.concatenate(slopes, axis=0)

    made = {}
    dk = dv = None
    for t in range(QUERY_HEADS + GROUP_HEADS):
        if t < QUERY_HEADS:
            made[t] = slopes_of(t)
        h = t - GROUP_HEADS
        if h < 0:
            continue
        low, slopes = made.pop(h)
        k = dot_nn(slopes, head(q, h))
        v = dot_nn(low, head(do, h))
        first = h % GROUP_HEADS == 0
        dk = k if first else dk + k
        dv = v if first else dv + v
        if h % GROUP_HEADS == GROUP_HEADS - 1:
            cols = columns[h // GROUP_HEADS]
            for b, out in zip(blocks, outs):
                out[0, :, cols] = (dk[b] * SCALE).astype(BF16)
                out[1, :, cols] = dv[b].astype(BF16)


def local_backward(
    q, do, kv, r1, r2, r3, p1, dp1, p2, dp2, w_in, ds_in, f_in, d_in,
    out, dq, drk, drv, own,
):
    near = SHARD + HALF
    far = near + REMOTE
    for g in range(KV_HEADS):
        cols = slice(g * HEAD_DIM, (g + 1) * HEAD_DIM)
        shards = (r1, r2, r3)
        k_t = jnp.concatenate(
            [kv[0, :near, cols]] + [r[0, :, cols] for r in shards] + [kv[0, near:, cols]], axis=0
        ).T
        v_t = jnp.concatenate(
            [kv[1, :near, cols]] + [r[1, :, cols] for r in shards] + [kv[1, near:, cols]], axis=0
        ).T
        dk1 = jnp.zeros((near, HEAD_DIM), F32)
        dv1 = jnp.zeros((near, HEAD_DIM), F32)
        dk2 = jnp.zeros((HALF, HEAD_DIM), F32)
        dv2 = jnp.zeros((HALF, HEAD_DIM), F32)
        for pair in range(GROUP_HEADS // 2):
            first = g * GROUP_HEADS + 2 * pair
            qs = [q[:, h * HEAD_DIM : (h + 1) * HEAD_DIM] for h in (first, first + 1)]
            ds = [do[:, h * HEAD_DIM : (h + 1) * HEAD_DIM] for h in (first, first + 1)]
            fs = [f_in[h : h + 1, :] for h in (first, first + 1)]
            cs = [d_in[h : h + 1, :] for h in (first, first + 1)]
            w2 = p2[first // 2] * halves(*fs)
            s2 = (w2 * (dp2[first // 2] - halves(*cs))).astype(BF16)
            w2 = w2.astype(BF16)
            dk2 = dk2 + dot_nn(s2, second_half(*qs))
            dv2 = dv2 + dot_nn(w2, second_half(*ds))
            o2 = dot_nn(v_t[:, far:], w2)
            dq2 = dot_nn(k_t[:, far:], s2)
            for i in range(2):
                h = first + i
                w1 = p1[h] * fs[i]
                s1 = (w1 * (dp1[h] - cs[i])).astype(BF16)
                w1 = w1.astype(BF16)
                dk1 = dk1 + dot_nn(s1, qs[i])
                dv1 = dv1 + dot_nn(w1, ds[i])
                half = slice(i * HALF, (i + 1) * HALF)
                o = dot_nn(v_t[:, :near], w1) + dot_nn(v_t[:, near:far], w_in[h])
                gq = dot_nn(k_t[:, :near], s1) + dot_nn(k_t[:, near:far], ds_in[h])
                o = jnp.concatenate([o[:, :HALF], o[:, HALF:] + o2[:, half]], axis=1)
                gq = jnp.concatenate([gq[:, :HALF], gq[:, HALF:] + dq2[:, half]], axis=1)
                out[:, h * HEAD_DIM : (h + 1) * HEAD_DIM] = o.T.astype(BF16)
                dq[:, h * HEAD_DIM : (h + 1) * HEAD_DIM] = (gq.T * SCALE).astype(BF16)
        dk1 = dk1 * SCALE
        own[0, :, cols] = dk1[:SHARD].astype(BF16)
        own[1, :, cols] = dv1[:SHARD].astype(BF16)
        drk[:HALF, cols] = dk1[SHARD:].astype(BF16)
        drv[:HALF, cols] = dv1[SHARD:].astype(BF16)
        drk[HALF:, cols] = (dk2 * SCALE).astype(BF16)
        drv[HALF:, cols] = dv2.astype(BF16)


def add_partials(a, b, c, d, keys, values):
    keys[...] = (
        (a[0].astype(F32) + b[0].astype(F32)) + (c[0].astype(F32) + d[0].astype(F32))
    ).astype(BF16)
    values[...] = (
        (a[1].astype(F32) + b[1].astype(F32)) + (c[1].astype(F32) + d[1].astype(F32))
    ).astype(BF16)


def in_vmem(x):
    return pltpu.with_memory_space_constraint(x, pltpu.VMEM)


def in_hbm(x):
    return pltpu.with_memory_space_constraint(x, pltpu.HBM)


def call(body, name, ins, outs, scratch=(), in_space=pltpu.VMEM, flops=0):
    return pl.pallas_call(
        body,
        name=name,
        in_specs=[pl.BlockSpec(memory_space=in_space)] * len(ins),
        out_specs=[pl.BlockSpec(memory_space=pltpu.VMEM)] * len(outs),
        out_shape=outs,
        scratch_shapes=list(scratch),
        cost_estimate=pl.CostEstimate(flops=flops, bytes_accessed=1 << 20, transcendentals=0),
        compiler_params=pltpu.CompilerParams(vmem_limit_bytes=24 * 1024 * 1024),
    )(*ins)


def per_device(
    query, response_keys, response_values, prompt_keys, prompt_values, dout, row_slot, row_pos
):
    devices = lax.axis_size("rows")
    stride = devices // GROUP
    hbm = jax.ShapeDtypeStruct
    width = KV_HEADS * HEAD_DIM
    heads = (QUERY_HEADS, ROWS)
    stacked = jnp.stack([prompt_keys, prompt_values])

    def moved(block, steps):
        route = [(i, (i + steps * stride) % devices) for i in range(devices)]
        return lax.ppermute(block, "rows", route)

    remote = [moved(stacked, steps) for steps in (1, 3, 2)]
    slot = row_slot.reshape(1, ROWS)
    pos = row_pos.reshape(1, ROWS)
    pair_heads = QUERY_HEADS // 2
    near = SHARD + HALF
    arrays = (
        query, dout, prompt_keys, prompt_values, response_keys, response_values, slot, pos
    )
    q, do, kv, p1, dp1, p2, dp2, m, l, c, live = map(
        in_vmem,
        call(
            local_forward,
            "local_forward",
            [in_hbm(x) for x in arrays],
            [
                VM(query.shape, BF16),
                VM(query.shape, BF16),
                VM((2, SHARD + ROWS, width), BF16),
                VM((QUERY_HEADS, near, ROWS), F32),
                VM((QUERY_HEADS, near, ROWS), F32),
                VM((pair_heads, HALF, ROWS), F32),
                VM((pair_heads, HALF, ROWS), F32),
                VM(heads, F32),
                VM(heads, F32),
                VM(heads, F32),
                VM((1, ROWS), F32),
            ],
            [
                VM((ROWS, ROWS), F32),
                VM((1, ROWS), jnp.int32),
                VM((1, ROWS), jnp.int32),
                pltpu.SemaphoreType.DMA((6 + 2 * KV_HEADS,)),
            ],
            in_space=pltpu.HBM,
            flops=10**9,
        ),
    )
    partial = (2, SHARD, width)
    w, ds, f, d, g1, g2, g3 = call(
        remote_pass,
        "remote_pass",
        [q, do, *remote, live, m, l, c],
        [
            VM((QUERY_HEADS, REMOTE, ROWS), BF16),
            VM((QUERY_HEADS, REMOTE, ROWS), BF16),
            VM(heads, F32),
            VM(heads, F32),
            hbm(partial, BF16),
            hbm(partial, BF16),
            hbm(partial, BF16),
        ],
        flops=2 * 10**9,
    )
    back = [moved(g, -steps) for g, steps in ((g1, 1), (g2, 3), (g3, 2))]
    out, dq, drk, drv, own = call(
        local_backward,
        "local_backward",
        [q, do, kv, *remote, p1, dp1, p2, dp2] + [in_vmem(x) for x in (w, ds, f, d)],
        [
            hbm(query.shape, BF16),
            hbm(query.shape, BF16),
            hbm(response_keys.shape, BF16),
            hbm(response_keys.shape, BF16),
            hbm(partial, BF16),
        ],
        flops=3 * 10**9,
    )
    gpk, gpv = call(
        add_partials,
        "add_partials",
        [own, *back],
        [hbm(prompt_keys.shape, BF16), hbm(prompt_keys.shape, BF16)],
    )
    return out, dq, drk, drv, gpk, gpv


def solution(mesh):
    rows = P("rows", None)
    return jax.shard_map(
        per_device,
        mesh=mesh,
        in_specs=(rows,) * 6 + (P("rows"),) * 2,
        out_specs=(rows,) * 6,
        check_vma=False,
    )
```

```python
import jax
import jax.numpy as jnp
from jax import lax
from jax.experimental import pallas as pl
from jax.experimental.pallas import tpu as pltpu
from jax.sharding import PartitionSpec as P

QUERY_HEADS = 16
KV_HEADS = 2
GROUP_HEADS = QUERY_HEADS // KV_HEADS
HEAD_DIM = 128
GROUP = 4
STEPS = (3, 1, 2)
SEND_ORDER = (0, 1, 2)
ROWS = 256
HALF = 128
SHARD = 128
REMOTE = (GROUP - 1) * SHARD
SCALE = HEAD_DIM**-0.5
EXP2_SCALE = SCALE * 1.4426950408889634
NEG = -1e30
LOAD_AT = (0, 4)
LATE_SKEW = 2
F32 = jnp.float32
BF16 = jnp.bfloat16
VM = pltpu.VMEM


def dot_nt(a, b):
    return lax.dot_general(a, b, (((1,), (1,)), ((), ())), preferred_element_type=F32)


def dot_nn(a, b):
    return lax.dot_general(a, b, (((1,), (0,)), ((), ())), preferred_element_type=F32)


def col_max(x):
    return jnp.max(x, axis=0, keepdims=True)


def col_sum(x):
    return jnp.sum(x, axis=0, keepdims=True)


def second_half(a, b):
    return jnp.concatenate([a[HALF:], b[HALF:]], axis=0)


def halves(a, b):
    return jnp.concatenate([a[:, HALF:], b[:, HALF:]], axis=1)


def unhalves(x, which, fill):
    return jnp.concatenate([fill, x[:, which * HALF : (which + 1) * HALF]], axis=1)


def local_forward(
    q_in, do_in, pk, pv, rk, rv, slot_in, pos_in,
    q, do, kv, p1, dp1, p2, dp2, m_out, l_out, c_out, live,
    bias, slot, pos, sems,
):
    pieces = [
        (slot_in, slot),
        (pos_in, pos),
        (pk, kv.at[0, pl.ds(0, SHARD)]),
        (rk, kv.at[0, pl.ds(SHARD, ROWS)]),
        (pv, kv.at[1, pl.ds(0, SHARD)]),
        (rv, kv.at[1, pl.ds(SHARD, ROWS)]),
    ]
    for n in range(QUERY_HEADS // 2):
        span = pl.ds(n * 2 * HEAD_DIM, 2 * HEAD_DIM)
        pieces.append((q_in.at[:, span], q.at[:, span]))
        pieces.append((do_in.at[:, span], do.at[:, span]))
    copies = [pltpu.make_async_copy(a, b, sems.at[n]) for n, (a, b) in enumerate(pieces)]
    for copy in copies:
        copy.start()
    copies[0].wait()
    copies[1].wait()
    slot_row = jnp.broadcast_to(slot[...], (ROWS, ROWS)).astype(F32)
    pos_row = jnp.broadcast_to(pos[...], (ROWS, ROWS)).astype(F32)
    slot_col = slot_row.T
    pos_col = pos_row.T
    seen = (slot_col == slot_row) & (slot_col >= 0) & (pos_col <= pos_row)
    bias[...] = jnp.where(seen, 0.0, NEG)
    live[...] = (slot[...] >= 0).astype(F32)
    nothing = jnp.full((1, HALF), NEG, F32)
    zero = jnp.zeros((1, HALF), F32)
    near = SHARD + HALF
    for copy in copies[2:6]:
        copy.wait()
    for g in range(KV_HEADS):
        cols = slice(g * HEAD_DIM, (g + 1) * HEAD_DIM)
        k1 = kv[0, :near, cols]
        v1 = kv[1, :near, cols]
        k2 = kv[0, near:, cols]
        v2 = kv[1, near:, cols]
        for pair in range(GROUP_HEADS // 2):
            first = g * GROUP_HEADS + 2 * pair
            if first in LOAD_AT:
                stop = min([n for n in LOAD_AT if n > first] + [QUERY_HEADS])
                for copy in copies[6 + first : 6 + stop]:
                    copy.wait()
            qs = [q[:, h * HEAD_DIM : (h + 1) * HEAD_DIM] for h in (first, first + 1)]
            ds = [do[:, h * HEAD_DIM : (h + 1) * HEAD_DIM] for h in (first, first + 1)]
            b2 = bias[HALF:, HALF:]
            s2 = dot_nt(k2, second_half(*qs)) + jnp.concatenate([b2, b2], axis=1)
            m2 = col_max(s2)
            ms, ls, cs = [], [], []
            for i in range(2):
                s1 = dot_nt(k1, qs[i])
                s1 = jnp.concatenate([s1[:SHARD], s1[SHARD:] + bias[:HALF, :]], axis=0)
                m = jnp.maximum(col_max(s1), unhalves(m2, i, nothing))
                e1 = jnp.exp2((s1 - m) * EXP2_SCALE)
                g1 = dot_nt(v1, ds[i])
                p1[first + i] = e1
                dp1[first + i] = g1
                ms.append(m)
                ls.append(col_sum(e1))
                cs.append(col_sum(e1 * g1))
            e2 = jnp.exp2((s2 - halves(*ms)) * EXP2_SCALE)
            g2 = dot_nt(v2, second_half(*ds))
            p2[first // 2] = e2
            dp2[first // 2] = g2
            l2 = col_sum(e2)
            c2 = col_sum(e2 * g2)
            for i in range(2):
                h = first + i
                m_out[h : h + 1, :] = ms[i]
                l_out[h : h + 1, :] = ls[i] + unhalves(l2, i, zero)
                c_out[h : h + 1, :] = cs[i] + unhalves(c2, i, zero)


def head(ref, h):
    return ref[:, h * HEAD_DIM : (h + 1) * HEAD_DIM]


def columns_of(h):
    g = h // GROUP_HEADS
    return slice(g * HEAD_DIM, (g + 1) * HEAD_DIM)


def block(n):
    return slice(n * SHARD, (n + 1) * SHARD)


def early_forward(q, do, rx, ry, m_in, l_in, c_in, e_out, p_out, tx, ty, m_out, l_out, c_out):
    for h in range(QUERY_HEADS):
        cols = columns_of(h)
        row = slice(h, h + 1)
        s = dot_nt(jnp.concatenate([rx[0, :, cols], ry[0, :, cols]], axis=0), head(q, h))
        pressure = dot_nt(jnp.concatenate([rx[1, :, cols], ry[1, :, cols]], axis=0), head(do, h))
        m_old = m_in[row, :]
        m = m_old
        tops, sums, centres = [], [], []
        for n in range(2):
            top = col_max(s[block(n)])
            e = jnp.exp2((s[block(n)] - top) * EXP2_SCALE)
            p = pressure[block(n)]
            e_out[h, block(n)] = e
            p_out[h, block(n)] = p
            tops.append(top)
            sums.append(col_sum(e))
            centres.append(col_sum(e * p))
            m = jnp.maximum(m, top)
        back = jnp.exp2((m_old - m) * EXP2_SCALE)
        total = l_in[row, :] * back
        centre = c_in[row, :] * back
        for top, a, b in zip(tops, sums, centres):
            factor = jnp.exp2((top - m) * EXP2_SCALE)
            total = total + a * factor
            centre = centre + b * factor
        tx[row, :] = tops[0]
        ty[row, :] = tops[1]
        m_out[row, :] = m
        l_out[row, :] = total
        c_out[row, :] = centre


def late_pass(
    q, do, rz, live, m_first, tx, ty, m_in, l_in, c_in, e_in, p_in,
    w_out, ds_out, f_out, d_out, gx, gy, gz,
):
    alive = live[...]

    def slopes_of(h):
        cols = columns_of(h)
        row = slice(h, h + 1)
        s = dot_nt(rz[0, :, cols], head(q, h))
        pressure = dot_nt(rz[1, :, cols], head(do, h))
        m_old = m_in[row, :]
        top = col_max(s)
        e = jnp.exp2((s - top) * EXP2_SCALE)
        m = jnp.maximum(m_old, top)
        back = jnp.exp2((m_old - m) * EXP2_SCALE)
        factor = jnp.exp2((top - m) * EXP2_SCALE)
        total = l_in[row, :] * back + col_sum(e) * factor
        inv = 1.0 / total
        centre = (c_in[row, :] * back + col_sum(e * pressure) * factor) * inv
        inv = inv * alive
        f_out[row, :] = jnp.exp2((m_first[row, :] - m) * EXP2_SCALE) * inv
        d_out[row, :] = centre
        lows, slopes = [], []
        for n, (a, b) in enumerate(
            ((e_in[h, block(0)], p_in[h, block(0)]), (e_in[h, block(1)], p_in[h, block(1)]), (e, pressure))
        ):
            if n < 2:
                factor = jnp.exp2(((tx, ty)[n][row, :] - m) * EXP2_SCALE)
            else:
                factor = jnp.exp2((top - m) * EXP2_SCALE)
            w = a * (factor * inv)
            lows.append(w.astype(BF16))
            slopes.append((w * (b - centre)).astype(BF16))
            for half in range(2):
                w_out[h, half, block(n)] = lows[-1][:, half * HALF : (half + 1) * HALF]
                ds_out[h, half, block(n)] = slopes[-1][:, half * HALF : (half + 1) * HALF]
        return jnp.concatenate(lows, axis=0), jnp.concatenate(slopes, axis=0)

    def store(cols, dk, dv):
        for n, out in enumerate((gx, gy, gz)):
            out[0, :, cols] = (dk[block(n)] * SCALE).astype(BF16)
            out[1, :, cols] = dv[block(n)].astype(BF16)

    skewed_terms(q, do, slopes_of, store, LATE_SKEW)


def skewed_terms(q, do, slopes_of, store, skew):
    made = {}
    dk = dv = None
    for t in range(QUERY_HEADS + skew):
        if t < QUERY_HEADS:
            made[t] = slopes_of(t)
        h = t - skew
        if h < 0:
            continue
        low, slopes = made.pop(h)
        k = dot_nn(slopes, head(q, h))
        v = dot_nn(low, head(do, h))
        first = h % GROUP_HEADS == 0
        dk = k if first else dk + k
        dv = v if first else dv + v
        if h % GROUP_HEADS == GROUP_HEADS - 1:
            store(columns_of(h), dk, dv)


def local_backward(
    q, do, kv, rx, ry, rz, p1, dp1, p2, dp2, w_in, ds_in, f_in, d_in,
    out_hbm, dq_hbm, drk_hbm, drv_hbm, own,
    out, dq, drk, drv, sems,
):
    started = []

    def send(buffer, target, cols):
        copy = pltpu.make_async_copy(buffer.at[:, cols], target.at[:, cols], sems.at[len(started)])
        copy.start()
        started.append(copy)

    near = SHARD + HALF
    unseen = jnp.zeros((HALF, HALF), BF16)
    for g in range(KV_HEADS):
        cols = slice(g * HEAD_DIM, (g + 1) * HEAD_DIM)
        shards = (rx, ry, rz)
        k_t = jnp.concatenate(
            [kv[0, :near, cols]] + [r[0, :, cols] for r in shards] + [kv[0, near:, cols]], axis=0
        ).T
        v_t = jnp.concatenate(
            [kv[1, :near, cols]] + [r[1, :, cols] for r in shards] + [kv[1, near:, cols]], axis=0
        ).T
        dk1 = jnp.zeros((near, HEAD_DIM), F32)
        dv1 = jnp.zeros((near, HEAD_DIM), F32)
        dk2 = jnp.zeros((HALF, HEAD_DIM), F32)
        dv2 = jnp.zeros((HALF, HEAD_DIM), F32)
        for pair in range(GROUP_HEADS // 2):
            first = g * GROUP_HEADS + 2 * pair
            qs = [q[:, h * HEAD_DIM : (h + 1) * HEAD_DIM] for h in (first, first + 1)]
            ds = [do[:, h * HEAD_DIM : (h + 1) * HEAD_DIM] for h in (first, first + 1)]
            fs = [f_in[h : h + 1, :] for h in (first, first + 1)]
            cs = [d_in[h : h + 1, :] for h in (first, first + 1)]
            w2 = p2[first // 2] * halves(*fs)
            s2 = (w2 * (dp2[first // 2] - halves(*cs))).astype(BF16)
            w2 = w2.astype(BF16)
            dk2 = dk2 + dot_nn(s2, second_half(*qs))
            dv2 = dv2 + dot_nn(w2, second_half(*ds))
            for i in range(2):
                h = first + i
                w1 = p1[h] * fs[i]
                s1 = (w1 * (dp1[h] - cs[i])).astype(BF16)
                w1 = w1.astype(BF16)
                dk1 = dk1 + dot_nn(s1, qs[i])
                dv1 = dv1 + dot_nn(w1, ds[i])
                half = slice(i * HALF, (i + 1) * HALF)
                ws = [w1, jnp.concatenate([w_in[h, 0], w_in[h, 1]], axis=1), jnp.concatenate([unseen, w2[:, half]], axis=1)]
                ss = [s1, jnp.concatenate([ds_in[h, 0], ds_in[h, 1]], axis=1), jnp.concatenate([unseen, s2[:, half]], axis=1)]
                o = dot_nn(v_t, jnp.concatenate(ws, axis=0))
                gq = dot_nn(k_t, jnp.concatenate(ss, axis=0))
                out[:, h * HEAD_DIM : (h + 1) * HEAD_DIM] = o.astype(BF16).T
                dq[:, h * HEAD_DIM : (h + 1) * HEAD_DIM] = (gq * SCALE).astype(BF16).T
        dk1 = dk1 * SCALE
        own[0, :, cols] = dk1[:SHARD].astype(BF16)
        own[1, :, cols] = dv1[:SHARD].astype(BF16)
        drk[:HALF, cols] = dk1[SHARD:].astype(BF16)
        drv[:HALF, cols] = dv1[SHARD:].astype(BF16)
        drk[HALF:, cols] = (dk2 * SCALE).astype(BF16)
        drv[HALF:, cols] = dv2.astype(BF16)
        wide = pl.ds(g * GROUP_HEADS * HEAD_DIM, GROUP_HEADS * HEAD_DIM)
        narrow = pl.ds(g * HEAD_DIM, HEAD_DIM)
        send(out, out_hbm, wide)
        send(dq, dq_hbm, wide)
        send(drk, drk_hbm, narrow)
        send(drv, drv_hbm, narrow)
    for copy in started:
        copy.wait()


def add_partials(a, b, c, d, keys, values):
    keys[...] = (
        (a[0].astype(F32) + b[0].astype(F32)) + (c[0].astype(F32) + d[0].astype(F32))
    ).astype(BF16)
    values[...] = (
        (a[1].astype(F32) + b[1].astype(F32)) + (c[1].astype(F32) + d[1].astype(F32))
    ).astype(BF16)


def in_vmem(x):
    return pltpu.with_memory_space_constraint(x, pltpu.VMEM)


def in_hbm(x):
    return pltpu.with_memory_space_constraint(x, pltpu.HBM)


def call(body, name, ins, outs, scratch=(), in_space=pltpu.VMEM, to_hbm=0, flops=0):
    return pl.pallas_call(
        body,
        name=name,
        in_specs=[pl.BlockSpec(memory_space=in_space)] * len(ins),
        out_specs=[pl.BlockSpec(memory_space=pltpu.HBM)] * to_hbm
        + [pl.BlockSpec(memory_space=pltpu.VMEM)] * (len(outs) - to_hbm),
        out_shape=outs,
        scratch_shapes=list(scratch),
        cost_estimate=pl.CostEstimate(flops=flops, bytes_accessed=1 << 20, transcendentals=0),
        compiler_params=pltpu.CompilerParams(vmem_limit_bytes=24 * 1024 * 1024),
    )(*ins)


def per_device(
    query, response_keys, response_values, prompt_keys, prompt_values, dout, row_slot, row_pos
):
    devices = lax.axis_size("rows")
    stride = devices // GROUP
    hbm = jax.ShapeDtypeStruct
    width = KV_HEADS * HEAD_DIM
    heads = (QUERY_HEADS, ROWS)
    stacked = jnp.stack([prompt_keys, prompt_values])

    def moved(block, steps):
        route = [(i, (i + steps * stride) % devices) for i in range(devices)]
        return lax.ppermute(block, "rows", route)

    remote = [moved(stacked, steps) for steps in STEPS]
    slot = row_slot.reshape(1, ROWS)
    pos = row_pos.reshape(1, ROWS)
    pair_heads = QUERY_HEADS // 2
    near = SHARD + HALF
    arrays = (
        query, dout, prompt_keys, prompt_values, response_keys, response_values, slot, pos
    )
    q, do, kv, p1, dp1, p2, dp2, m, l, c, live = map(
        in_vmem,
        call(
            local_forward,
            "local_forward",
            [in_hbm(x) for x in arrays],
            [
                VM(query.shape, BF16),
                VM(query.shape, BF16),
                VM((2, SHARD + ROWS, width), BF16),
                VM((QUERY_HEADS, near, ROWS), F32),
                VM((QUERY_HEADS, near, ROWS), F32),
                VM((pair_heads, HALF, ROWS), F32),
                VM((pair_heads, HALF, ROWS), F32),
                VM(heads, F32),
                VM(heads, F32),
                VM(heads, F32),
                VM((1, ROWS), F32),
            ],
            [
                VM((ROWS, ROWS), F32),
                VM((1, ROWS), jnp.int32),
                VM((1, ROWS), jnp.int32),
                pltpu.SemaphoreType.DMA((6 + QUERY_HEADS,)),
            ],
            in_space=pltpu.HBM,
            flops=10**9,
        ),
    )
    partial = (2, SHARD, width)
    rx, ry, rz = remote
    early = (QUERY_HEADS, 2 * SHARD, ROWS)
    every = (QUERY_HEADS, ROWS // HALF, REMOTE, HALF)
    e, p, tx, ty, m2, l2, c2 = map(
        in_vmem,
        call(
            early_forward,
            "early_forward",
            [q, do, rx, ry, m, l, c],
            [VM(early, F32)] * 2 + [VM(heads, F32)] * 5,
            flops=10**9,
        ),
    )
    w, ds, f, d, *terms = call(
        late_pass,
        "late_pass",
        [q, do, rz, live, m, tx, ty, m2, l2, c2, e, p],
        [VM(every, BF16)] * 2 + [VM(heads, F32)] * 2 + [hbm(partial, BF16)] * 3,
        flops=10**9,
    )
    back = [moved(terms[n], -STEPS[n]) for n in SEND_ORDER]
    out, dq, drk, drv, own = call(
        local_backward,
        "local_backward",
        [q, do, kv, *remote, p1, dp1, p2, dp2] + [in_vmem(x) for x in (w, ds, f, d)],
        [
            hbm(query.shape, BF16),
            hbm(query.shape, BF16),
            hbm(response_keys.shape, BF16),
            hbm(response_keys.shape, BF16),
            hbm(partial, BF16),
        ],
        [
            VM(query.shape, BF16),
            VM(query.shape, BF16),
            VM(response_keys.shape, BF16),
            VM(response_keys.shape, BF16),
            pltpu.SemaphoreType.DMA((4 * KV_HEADS,)),
        ],
        to_hbm=4,
        flops=10**6,
    )
    gpk, gpv = call(
        add_partials,
        "add_partials",
        [own, *back],
        [hbm(prompt_keys.shape, BF16), hbm(prompt_keys.shape, BF16)],
    )
    return out, dq, drk, drv, gpk, gpv


def solution(mesh):
    rows = P("rows", None)
    return jax.shard_map(
        per_device,
        mesh=mesh,
        in_specs=(rows,) * 6 + (P("rows"),) * 2,
        out_specs=(rows,) * 6,
        check_vma=False,
    )
```

```python
import jax
import jax.numpy as jnp
from jax import lax
from jax.experimental import pallas as pl
from jax.experimental.pallas import tpu as pltpu
from jax.sharding import PartitionSpec as P

QUERY_HEADS = 16
KV_HEADS = 2
GROUP_HEADS = QUERY_HEADS // KV_HEADS
HEAD_DIM = 128
GROUP = 4
STEPS = (3, 1, 2)
SEND_ORDER = (0, 1, 2)
ROWS = 256
HALF = 128
SHARD = 128
REMOTE = (GROUP - 1) * SHARD
SCALE = HEAD_DIM**-0.5
EXP2_SCALE = SCALE * 1.4426950408889634
NEG = -1e30
LOAD_AT = (0, 4)
LATE_SKEW = 2
F32 = jnp.float32
BF16 = jnp.bfloat16
VM = pltpu.VMEM


def dot_nt(a, b):
    return lax.dot_general(a, b, (((1,), (1,)), ((), ())), preferred_element_type=F32)


def dot_nn(a, b):
    return lax.dot_general(a, b, (((1,), (0,)), ((), ())), preferred_element_type=F32)


def col_max(x):
    return jnp.max(x, axis=0, keepdims=True)


def col_sum(x):
    return jnp.sum(x, axis=0, keepdims=True)


def second_half(a, b):
    return jnp.concatenate([a[HALF:], b[HALF:]], axis=0)


def halves(a, b):
    return jnp.concatenate([a[:, HALF:], b[:, HALF:]], axis=1)


def unhalves(x, which, fill):
    return jnp.concatenate([fill, x[:, which * HALF : (which + 1) * HALF]], axis=1)


def local_forward(
    q_in, do_in, pk, pv, rk, rv, slot_in, pos_in,
    q, do, kv, p1, dp1, p2, dp2, m_out, l_out, c_out, live,
    bias, slot, pos, sems,
):
    pieces = [
        (slot_in, slot),
        (pos_in, pos),
        (pk, kv.at[0, pl.ds(0, SHARD)]),
        (rk, kv.at[0, pl.ds(SHARD, ROWS)]),
        (pv, kv.at[1, pl.ds(0, SHARD)]),
        (rv, kv.at[1, pl.ds(SHARD, ROWS)]),
    ]
    for h in range(QUERY_HEADS):
        span = pl.ds(h * HEAD_DIM, HEAD_DIM)
        pieces.append((q_in.at[:, span], q.at[h]))
        pieces.append((do_in.at[:, span], do.at[h]))
    copies = [pltpu.make_async_copy(a, b, sems.at[n]) for n, (a, b) in enumerate(pieces)]
    for copy in copies:
        copy.start()
    copies[0].wait()
    copies[1].wait()
    slot_row = jnp.broadcast_to(slot[...], (ROWS, ROWS)).astype(F32)
    pos_row = jnp.broadcast_to(pos[...], (ROWS, ROWS)).astype(F32)
    slot_col = slot_row.T
    pos_col = pos_row.T
    seen = (slot_col == slot_row) & (slot_col >= 0) & (pos_col <= pos_row)
    bias[...] = jnp.where(seen, 0.0, NEG)
    live[...] = (slot[...] >= 0).astype(F32)
    nothing = jnp.full((1, HALF), NEG, F32)
    zero = jnp.zeros((1, HALF), F32)
    near = SHARD + HALF
    for copy in copies[2:6]:
        copy.wait()
    for g in range(KV_HEADS):
        cols = slice(g * HEAD_DIM, (g + 1) * HEAD_DIM)
        k1 = kv[0, :near, cols]
        v1 = kv[1, :near, cols]
        k2 = kv[0, near:, cols]
        v2 = kv[1, near:, cols]
        for pair in range(GROUP_HEADS // 2):
            first = g * GROUP_HEADS + 2 * pair
            if first in LOAD_AT:
                stop = min([n for n in LOAD_AT if n > first] + [QUERY_HEADS])
                for copy in copies[6 + 2 * first : 6 + 2 * stop]:
                    copy.wait()
            qs = [head(q, h) for h in (first, first + 1)]
            ds = [head(do, h) for h in (first, first + 1)]
            b2 = bias[HALF:, HALF:]
            s2 = dot_nt(k2, second_half(*qs)) + jnp.concatenate([b2, b2], axis=1)
            m2 = col_max(s2)
            ms, ls, cs = [], [], []
            for i in range(2):
                s1 = dot_nt(k1, qs[i])
                s1 = jnp.concatenate([s1[:SHARD], s1[SHARD:] + bias[:HALF, :]], axis=0)
                m = jnp.maximum(col_max(s1), unhalves(m2, i, nothing))
                e1 = jnp.exp2((s1 - m) * EXP2_SCALE)
                g1 = dot_nt(v1, ds[i])
                p1[first + i] = e1
                dp1[first + i] = g1
                ms.append(m)
                ls.append(col_sum(e1))
                cs.append(col_sum(e1 * g1))
            e2 = jnp.exp2((s2 - halves(*ms)) * EXP2_SCALE)
            g2 = dot_nt(v2, second_half(*ds))
            p2[first // 2] = e2
            dp2[first // 2] = g2
            l2 = col_sum(e2)
            c2 = col_sum(e2 * g2)
            for i in range(2):
                h = first + i
                m_out[h : h + 1, :] = ms[i]
                l_out[h : h + 1, :] = ls[i] + unhalves(l2, i, zero)
                c_out[h : h + 1, :] = cs[i] + unhalves(c2, i, zero)


def head(ref, h):
    return ref[h]


def columns_of(h):
    g = h // GROUP_HEADS
    return slice(g * HEAD_DIM, (g + 1) * HEAD_DIM)


def block(n):
    return slice(n * SHARD, (n + 1) * SHARD)


def early_forward(q, do, rx, ry, m_in, l_in, c_in, e_out, p_out, tx, ty, m_out, l_out, c_out):
    for h in range(QUERY_HEADS):
        cols = columns_of(h)
        row = slice(h, h + 1)
        s = dot_nt(jnp.concatenate([rx[0, :, cols], ry[0, :, cols]], axis=0), head(q, h))
        pressure = dot_nt(jnp.concatenate([rx[1, :, cols], ry[1, :, cols]], axis=0), head(do, h))
        m_old = m_in[row, :]
        m = m_old
        tops, sums, centres = [], [], []
        for n in range(2):
            top = col_max(s[block(n)])
            e = jnp.exp2((s[block(n)] - top) * EXP2_SCALE)
            p = pressure[block(n)]
            e_out[h, block(n)] = e
            p_out[h, block(n)] = p
            tops.append(top)
            sums.append(col_sum(e))
            centres.append(col_sum(e * p))
            m = jnp.maximum(m, top)
        back = jnp.exp2((m_old - m) * EXP2_SCALE)
        total = l_in[row, :] * back
        centre = c_in[row, :] * back
        for top, a, b in zip(tops, sums, centres):
            factor = jnp.exp2((top - m) * EXP2_SCALE)
            total = total + a * factor
            centre = centre + b * factor
        tx[row, :] = tops[0]
        ty[row, :] = tops[1]
        m_out[row, :] = m
        l_out[row, :] = total
        c_out[row, :] = centre


def late_pass(
    q, do, rz, live, m_first, tx, ty, m_in, l_in, c_in, e_in, p_in,
    w_out, ds_out, f_out, d_out, gx, gy, gz,
):
    alive = live[...]

    def slopes_of(h):
        cols = columns_of(h)
        row = slice(h, h + 1)
        s = dot_nt(rz[0, :, cols], head(q, h))
        pressure = dot_nt(rz[1, :, cols], head(do, h))
        m_old = m_in[row, :]
        top = col_max(s)
        e = jnp.exp2((s - top) * EXP2_SCALE)
        m = jnp.maximum(m_old, top)
        back = jnp.exp2((m_old - m) * EXP2_SCALE)
        factor = jnp.exp2((top - m) * EXP2_SCALE)
        total = l_in[row, :] * back + col_sum(e) * factor
        inv = 1.0 / total
        centre = (c_in[row, :] * back + col_sum(e * pressure) * factor) * inv
        inv = inv * alive
        f_out[row, :] = jnp.exp2((m_first[row, :] - m) * EXP2_SCALE) * inv
        d_out[row, :] = centre
        lows, slopes = [], []
        for n, (a, b) in enumerate(
            ((e_in[h, block(0)], p_in[h, block(0)]), (e_in[h, block(1)], p_in[h, block(1)]), (e, pressure))
        ):
            if n < 2:
                factor = jnp.exp2(((tx, ty)[n][row, :] - m) * EXP2_SCALE)
            else:
                factor = jnp.exp2((top - m) * EXP2_SCALE)
            w = a * (factor * inv)
            lows.append(w.astype(BF16))
            slopes.append((w * (b - centre)).astype(BF16))
            for half in range(2):
                w_out[h, half, block(n)] = lows[-1][:, half * HALF : (half + 1) * HALF]
                ds_out[h, half, block(n)] = slopes[-1][:, half * HALF : (half + 1) * HALF]
        return jnp.concatenate(lows, axis=0), jnp.concatenate(slopes, axis=0)

    def store(cols, dk, dv):
        for n, out in enumerate((gx, gy, gz)):
            out[0, :, cols] = (dk[block(n)] * SCALE).astype(BF16)
            out[1, :, cols] = dv[block(n)].astype(BF16)

    skewed_terms(q, do, slopes_of, store, LATE_SKEW)


def skewed_terms(q, do, slopes_of, store, skew):
    made = {}
    dk = dv = None
    for t in range(QUERY_HEADS + skew):
        if t < QUERY_HEADS:
            made[t] = slopes_of(t)
        h = t - skew
        if h < 0:
            continue
        low, slopes = made.pop(h)
        k = dot_nn(slopes, head(q, h))
        v = dot_nn(low, head(do, h))
        first = h % GROUP_HEADS == 0
        dk = k if first else dk + k
        dv = v if first else dv + v
        if h % GROUP_HEADS == GROUP_HEADS - 1:
            store(columns_of(h), dk, dv)


def local_backward(
    q, do, kv, rx, ry, rz, p1, dp1, p2, dp2, w_in, ds_in, f_in, d_in,
    out_hbm, dq_hbm, drk_hbm, drv_hbm, own,
    out, dq, drk, drv, sems,
):
    started = []

    def send(buffer, target, cols):
        copy = pltpu.make_async_copy(buffer.at[:, cols], target.at[:, cols], sems.at[len(started)])
        copy.start()
        started.append(copy)

    near = SHARD + HALF
    unseen = jnp.zeros((HALF, HALF), BF16)
    for g in range(KV_HEADS):
        cols = slice(g * HEAD_DIM, (g + 1) * HEAD_DIM)
        shards = (rx, ry, rz)
        k_t = jnp.concatenate(
            [kv[0, :near, cols]] + [r[0, :, cols] for r in shards] + [kv[0, near:, cols]], axis=0
        ).T
        v_t = jnp.concatenate(
            [kv[1, :near, cols]] + [r[1, :, cols] for r in shards] + [kv[1, near:, cols]], axis=0
        ).T
        dk1 = jnp.zeros((near, HEAD_DIM), F32)
        dv1 = jnp.zeros((near, HEAD_DIM), F32)
        dk2 = jnp.zeros((HALF, HEAD_DIM), F32)
        dv2 = jnp.zeros((HALF, HEAD_DIM), F32)
        for pair in range(GROUP_HEADS // 2):
            first = g * GROUP_HEADS + 2 * pair
            qs = [head(q, h) for h in (first, first + 1)]
            ds = [head(do, h) for h in (first, first + 1)]
            fs = [f_in[h : h + 1, :] for h in (first, first + 1)]
            cs = [d_in[h : h + 1, :] for h in (first, first + 1)]
            w2 = p2[first // 2] * halves(*fs)
            s2 = (w2 * (dp2[first // 2] - halves(*cs))).astype(BF16)
            w2 = w2.astype(BF16)
            dk2 = dk2 + dot_nn(s2, second_half(*qs))
            dv2 = dv2 + dot_nn(w2, second_half(*ds))
            for i in range(2):
                h = first + i
                w1 = p1[h] * fs[i]
                s1 = (w1 * (dp1[h] - cs[i])).astype(BF16)
                w1 = w1.astype(BF16)
                dk1 = dk1 + dot_nn(s1, qs[i])
                dv1 = dv1 + dot_nn(w1, ds[i])
                half = slice(i * HALF, (i + 1) * HALF)
                ws = [w1, jnp.concatenate([w_in[h, 0], w_in[h, 1]], axis=1), jnp.concatenate([unseen, w2[:, half]], axis=1)]
                ss = [s1, jnp.concatenate([ds_in[h, 0], ds_in[h, 1]], axis=1), jnp.concatenate([unseen, s2[:, half]], axis=1)]
                o = dot_nn(v_t, jnp.concatenate(ws, axis=0))
                gq = dot_nn(k_t, jnp.concatenate(ss, axis=0))
                out[:, h * HEAD_DIM : (h + 1) * HEAD_DIM] = o.astype(BF16).T
                dq[:, h * HEAD_DIM : (h + 1) * HEAD_DIM] = (gq * SCALE).astype(BF16).T
        dk1 = dk1 * SCALE
        own[0, :, cols] = dk1[:SHARD].astype(BF16)
        own[1, :, cols] = dv1[:SHARD].astype(BF16)
        drk[:HALF, cols] = dk1[SHARD:].astype(BF16)
        drv[:HALF, cols] = dv1[SHARD:].astype(BF16)
        drk[HALF:, cols] = (dk2 * SCALE).astype(BF16)
        drv[HALF:, cols] = dv2.astype(BF16)
        wide = pl.ds(g * GROUP_HEADS * HEAD_DIM, GROUP_HEADS * HEAD_DIM)
        narrow = pl.ds(g * HEAD_DIM, HEAD_DIM)
        send(out, out_hbm, wide)
        send(dq, dq_hbm, wide)
        send(drk, drk_hbm, narrow)
        send(drv, drv_hbm, narrow)
    for copy in started:
        copy.wait()


def add_partials(a, b, c, d, keys, values):
    keys[...] = (
        (a[0].astype(F32) + b[0].astype(F32)) + (c[0].astype(F32) + d[0].astype(F32))
    ).astype(BF16)
    values[...] = (
        (a[1].astype(F32) + b[1].astype(F32)) + (c[1].astype(F32) + d[1].astype(F32))
    ).astype(BF16)


def in_vmem(x):
    return pltpu.with_memory_space_constraint(x, pltpu.VMEM)


def in_hbm(x):
    return pltpu.with_memory_space_constraint(x, pltpu.HBM)


def call(body, name, ins, outs, scratch=(), in_space=pltpu.VMEM, to_hbm=0, flops=0):
    return pl.pallas_call(
        body,
        name=name,
        in_specs=[pl.BlockSpec(memory_space=in_space)] * len(ins),
        out_specs=[pl.BlockSpec(memory_space=pltpu.HBM)] * to_hbm
        + [pl.BlockSpec(memory_space=pltpu.VMEM)] * (len(outs) - to_hbm),
        out_shape=outs,
        scratch_shapes=list(scratch),
        cost_estimate=pl.CostEstimate(flops=flops, bytes_accessed=1 << 20, transcendentals=0),
        compiler_params=pltpu.CompilerParams(vmem_limit_bytes=24 * 1024 * 1024),
    )(*ins)


def per_device(
    query, response_keys, response_values, prompt_keys, prompt_values, dout, row_slot, row_pos
):
    devices = lax.axis_size("rows")
    stride = devices // GROUP
    hbm = jax.ShapeDtypeStruct
    width = KV_HEADS * HEAD_DIM
    heads = (QUERY_HEADS, ROWS)
    stacked = jnp.stack([prompt_keys, prompt_values])

    def moved(block, steps):
        route = [(i, (i + steps * stride) % devices) for i in range(devices)]
        return lax.ppermute(block, "rows", route)

    remote = [moved(stacked, steps) for steps in STEPS]
    slot = row_slot.reshape(1, ROWS)
    pos = row_pos.reshape(1, ROWS)
    pair_heads = QUERY_HEADS // 2
    near = SHARD + HALF
    arrays = (
        query, dout, prompt_keys, prompt_values, response_keys, response_values, slot, pos
    )
    q, do, kv, p1, dp1, p2, dp2, m, l, c, live = map(
        in_vmem,
        call(
            local_forward,
            "local_forward",
            [in_hbm(x) for x in arrays],
            [
                VM((QUERY_HEADS, ROWS, HEAD_DIM), BF16),
                VM((QUERY_HEADS, ROWS, HEAD_DIM), BF16),
                VM((2, SHARD + ROWS, width), BF16),
                VM((QUERY_HEADS, near, ROWS), F32),
                VM((QUERY_HEADS, near, ROWS), F32),
                VM((pair_heads, HALF, ROWS), F32),
                VM((pair_heads, HALF, ROWS), F32),
                VM(heads, F32),
                VM(heads, F32),
                VM(heads, F32),
                VM((1, ROWS), F32),
            ],
            [
                VM((ROWS, ROWS), F32),
                VM((1, ROWS), jnp.int32),
                VM((1, ROWS), jnp.int32),
                pltpu.SemaphoreType.DMA((6 + 2 * QUERY_HEADS,)),
            ],
            in_space=pltpu.HBM,
            flops=10**9,
        ),
    )
    partial = (2, SHARD, width)
    rx, ry, rz = remote
    early = (QUERY_HEADS, 2 * SHARD, ROWS)
    every = (QUERY_HEADS, ROWS // HALF, REMOTE, HALF)
    e, p, tx, ty, m2, l2, c2 = map(
        in_vmem,
        call(
            early_forward,
            "early_forward",
            [q, do, rx, ry, m, l, c],
            [VM(early, F32)] * 2 + [VM(heads, F32)] * 5,
            flops=10**9,
        ),
    )
    w, ds, f, d, *terms = call(
        late_pass,
        "late_pass",
        [q, do, rz, live, m, tx, ty, m2, l2, c2, e, p],
        [VM(every, BF16)] * 2 + [VM(heads, F32)] * 2 + [hbm(partial, BF16)] * 3,
        flops=10**9,
    )
    back = [moved(terms[n], -STEPS[n]) for n in SEND_ORDER]
    out, dq, drk, drv, own = call(
        local_backward,
        "local_backward",
        [q, do, kv, *remote, p1, dp1, p2, dp2] + [in_vmem(x) for x in (w, ds, f, d)],
        [
            hbm(query.shape, BF16),
            hbm(query.shape, BF16),
            hbm(response_keys.shape, BF16),
            hbm(response_keys.shape, BF16),
            hbm(partial, BF16),
        ],
        [
            VM(query.shape, BF16),
            VM(query.shape, BF16),
            VM(response_keys.shape, BF16),
            VM(response_keys.shape, BF16),
            pltpu.SemaphoreType.DMA((4 * KV_HEADS,)),
        ],
        to_hbm=4,
        flops=10**6,
    )
    gpk, gpv = call(
        add_partials,
        "add_partials",
        [own, *back],
        [hbm(prompt_keys.shape, BF16), hbm(prompt_keys.shape, BF16)],
    )
    return out, dq, drk, drv, gpk, gpv


def solution(mesh):
    rows = P("rows", None)
    return jax.shard_map(
        per_device,
        mesh=mesh,
        in_specs=(rows,) * 6 + (P("rows"),) * 2,
        out_specs=(rows,) * 6,
        check_vma=False,
    )
```

```python
import jax
import jax.numpy as jnp
from jax import lax
from jax.experimental import pallas as pl
from jax.experimental.pallas import tpu as pltpu
from jax.sharding import PartitionSpec as P

QUERY_HEADS = 16
KV_HEADS = 2
GROUP_HEADS = QUERY_HEADS // KV_HEADS
HEAD_DIM = 128
GROUP = 4
STEPS = (3, 1, 2)
SEND_ORDER = (0, 1, 2)
ROWS = 256
HALF = 128
SHARD = 128
REMOTE = (GROUP - 1) * SHARD
SCALE = HEAD_DIM**-0.5
EXP2_SCALE = SCALE * 1.4426950408889634
NEG = -1e30
LOAD_AT = (0, 4)
LATE_SKEW = 2
F32 = jnp.float32
BF16 = jnp.bfloat16
VM = pltpu.VMEM


def dot_nt(a, b):
    return lax.dot_general(a, b, (((1,), (1,)), ((), ())), preferred_element_type=F32)


def dot_nn(a, b):
    return lax.dot_general(a, b, (((1,), (0,)), ((), ())), preferred_element_type=F32)


def col_max(x):
    return jnp.max(x, axis=0, keepdims=True)


def col_sum(x):
    return jnp.sum(x, axis=0, keepdims=True)


def second_half(a, b):
    return jnp.concatenate([a[HALF:], b[HALF:]], axis=0)


def halves(a, b):
    return jnp.concatenate([a[:, HALF:], b[:, HALF:]], axis=1)


def unhalves(x, which, fill):
    return jnp.concatenate([fill, x[:, which * HALF : (which + 1) * HALF]], axis=1)


def local_forward(
    q_in, do_in, pk, pv, rk, rv, slot_in, pos_in,
    q, do, kv, p1, dp1, p2, dp2, m_out, l_out, c_out, live,
    bias, slot, pos, sems,
):
    pieces = [
        (slot_in, slot),
        (pos_in, pos),
    ]
    for g in range(KV_HEADS):
        cols = pl.ds(g * HEAD_DIM, HEAD_DIM)
        for n, (shard, rows) in enumerate(((pk, rk), (pv, rv))):
            pieces.append((shard.at[:, cols], kv.at[n, g, pl.ds(0, SHARD)]))
            pieces.append((rows.at[:, cols], kv.at[n, g, pl.ds(SHARD, ROWS)]))
    for h in range(QUERY_HEADS):
        span = pl.ds(h * HEAD_DIM, HEAD_DIM)
        pieces.append((q_in.at[:, span], q.at[h]))
        pieces.append((do_in.at[:, span], do.at[h]))
    copies = [pltpu.make_async_copy(a, b, sems.at[n]) for n, (a, b) in enumerate(pieces)]
    for copy in copies:
        copy.start()
    copies[0].wait()
    copies[1].wait()
    slot_row = jnp.broadcast_to(slot[...], (ROWS, ROWS)).astype(F32)
    pos_row = jnp.broadcast_to(pos[...], (ROWS, ROWS)).astype(F32)
    slot_col = slot_row.T
    pos_col = pos_row.T
    seen = (slot_col == slot_row) & (slot_col >= 0) & (pos_col <= pos_row)
    bias[...] = jnp.where(seen, 0.0, NEG)
    live[...] = (slot[...] >= 0).astype(F32)
    nothing = jnp.full((1, HALF), NEG, F32)
    zero = jnp.zeros((1, HALF), F32)
    near = SHARD + HALF
    for copy in copies[2:10]:
        copy.wait()
    for g in range(KV_HEADS):
        cols = slice(g * HEAD_DIM, (g + 1) * HEAD_DIM)
        k1 = kv[0, g, :near]
        v1 = kv[1, g, :near]
        k2 = kv[0, g, near:]
        v2 = kv[1, g, near:]
        for pair in range(GROUP_HEADS // 2):
            first = g * GROUP_HEADS + 2 * pair
            if first in LOAD_AT:
                stop = min([n for n in LOAD_AT if n > first] + [QUERY_HEADS])
                for copy in copies[10 + 2 * first : 10 + 2 * stop]:
                    copy.wait()
            qs = [head(q, h) for h in (first, first + 1)]
            ds = [head(do, h) for h in (first, first + 1)]
            b2 = bias[HALF:, HALF:]
            s2 = dot_nt(k2, second_half(*qs)) + jnp.concatenate([b2, b2], axis=1)
            m2 = col_max(s2)
            ms, ls, cs = [], [], []
            for i in range(2):
                s1 = dot_nt(k1, qs[i])
                s1 = jnp.concatenate([s1[:SHARD], s1[SHARD:] + bias[:HALF, :]], axis=0)
                m = jnp.maximum(col_max(s1), unhalves(m2, i, nothing))
                e1 = jnp.exp2((s1 - m) * EXP2_SCALE)
                g1 = dot_nt(v1, ds[i])
                p1[first + i] = e1
                dp1[first + i] = g1
                ms.append(m)
                ls.append(col_sum(e1))
                cs.append(col_sum(e1 * g1))
            e2 = jnp.exp2((s2 - halves(*ms)) * EXP2_SCALE)
            g2 = dot_nt(v2, second_half(*ds))
            p2[first // 2] = e2
            dp2[first // 2] = g2
            l2 = col_sum(e2)
            c2 = col_sum(e2 * g2)
            for i in range(2):
                h = first + i
                m_out[h : h + 1, :] = ms[i]
                l_out[h : h + 1, :] = ls[i] + unhalves(l2, i, zero)
                c_out[h : h + 1, :] = cs[i] + unhalves(c2, i, zero)


def head(ref, h):
    return ref[h]


def columns_of(h):
    g = h // GROUP_HEADS
    return slice(g * HEAD_DIM, (g + 1) * HEAD_DIM)


def block(n):
    return slice(n * SHARD, (n + 1) * SHARD)


def early_forward(q, do, rx, ry, m_in, l_in, c_in, e_out, p_out, tx, ty, m_out, l_out, c_out):
    for h in range(QUERY_HEADS):
        cols = columns_of(h)
        row = slice(h, h + 1)
        s = dot_nt(jnp.concatenate([rx[0, :, cols], ry[0, :, cols]], axis=0), head(q, h))
        pressure = dot_nt(jnp.concatenate([rx[1, :, cols], ry[1, :, cols]], axis=0), head(do, h))
        m_old = m_in[row, :]
        m = m_old
        tops, sums, centres = [], [], []
        for n in range(2):
            top = col_max(s[block(n)])
            e = jnp.exp2((s[block(n)] - top) * EXP2_SCALE)
            p = pressure[block(n)]
            e_out[h, block(n)] = e
            p_out[h, block(n)] = p
            tops.append(top)
            sums.append(col_sum(e))
            centres.append(col_sum(e * p))
            m = jnp.maximum(m, top)
        back = jnp.exp2((m_old - m) * EXP2_SCALE)
        total = l_in[row, :] * back
        centre = c_in[row, :] * back
        for top, a, b in zip(tops, sums, centres):
            factor = jnp.exp2((top - m) * EXP2_SCALE)
            total = total + a * factor
            centre = centre + b * factor
        tx[row, :] = tops[0]
        ty[row, :] = tops[1]
        m_out[row, :] = m
        l_out[row, :] = total
        c_out[row, :] = centre


def late_pass(
    q, do, rz, live, m_first, tx, ty, m_in, l_in, c_in, e_in, p_in,
    w_out, ds_out, f_out, d_out, gx, gy, gz,
):
    alive = live[...]

    def slopes_of(h):
        cols = columns_of(h)
        row = slice(h, h + 1)
        s = dot_nt(rz[0, :, cols], head(q, h))
        pressure = dot_nt(rz[1, :, cols], head(do, h))
        m_old = m_in[row, :]
        top = col_max(s)
        e = jnp.exp2((s - top) * EXP2_SCALE)
        m = jnp.maximum(m_old, top)
        back = jnp.exp2((m_old - m) * EXP2_SCALE)
        factor = jnp.exp2((top - m) * EXP2_SCALE)
        total = l_in[row, :] * back + col_sum(e) * factor
        inv = 1.0 / total
        centre = (c_in[row, :] * back + col_sum(e * pressure) * factor) * inv
        inv = inv * alive
        f_out[row, :] = jnp.exp2((m_first[row, :] - m) * EXP2_SCALE) * inv
        d_out[row, :] = centre
        lows, slopes = [], []
        for n, (a, b) in enumerate(
            ((e_in[h, block(0)], p_in[h, block(0)]), (e_in[h, block(1)], p_in[h, block(1)]), (e, pressure))
        ):
            if n < 2:
                factor = jnp.exp2(((tx, ty)[n][row, :] - m) * EXP2_SCALE)
            else:
                factor = jnp.exp2((top - m) * EXP2_SCALE)
            w = a * (factor * inv)
            lows.append(w.astype(BF16))
            slopes.append((w * (b - centre)).astype(BF16))
            for half in range(2):
                w_out[h, half, block(n)] = lows[-1][:, half * HALF : (half + 1) * HALF]
                ds_out[h, half, block(n)] = slopes[-1][:, half * HALF : (half + 1) * HALF]
        return jnp.concatenate(lows, axis=0), jnp.concatenate(slopes, axis=0)

    def store(cols, dk, dv):
        for n, out in enumerate((gx, gy, gz)):
            out[0, :, cols] = (dk[block(n)] * SCALE).astype(BF16)
            out[1, :, cols] = dv[block(n)].astype(BF16)

    skewed_terms(q, do, slopes_of, store, LATE_SKEW)


def skewed_terms(q, do, slopes_of, store, skew):
    made = {}
    dk = dv = None
    for t in range(QUERY_HEADS + skew):
        if t < QUERY_HEADS:
            made[t] = slopes_of(t)
        h = t - skew
        if h < 0:
            continue
        low, slopes = made.pop(h)
        k = dot_nn(slopes, head(q, h))
        v = dot_nn(low, head(do, h))
        first = h % GROUP_HEADS == 0
        dk = k if first else dk + k
        dv = v if first else dv + v
        if h % GROUP_HEADS == GROUP_HEADS - 1:
            store(columns_of(h), dk, dv)


def local_backward(
    q, do, kv, rx, ry, rz, p1, dp1, p2, dp2, w_in, ds_in, f_in, d_in,
    out_hbm, dq_hbm, drk_hbm, drv_hbm, own,
    out, dq, drk, drv, sems,
):
    started = []

    def send(buffer, target, cols):
        copy = pltpu.make_async_copy(buffer.at[:, cols], target.at[:, cols], sems.at[len(started)])
        copy.start()
        started.append(copy)

    near = SHARD + HALF
    unseen = jnp.zeros((HALF, HALF), BF16)
    for g in range(KV_HEADS):
        cols = slice(g * HEAD_DIM, (g + 1) * HEAD_DIM)
        shards = (rx, ry, rz)
        k_t = jnp.concatenate(
            [kv[0, g, :near]] + [r[0, :, cols] for r in shards] + [kv[0, g, near:]], axis=0
        ).T
        v_t = jnp.concatenate(
            [kv[1, g, :near]] + [r[1, :, cols] for r in shards] + [kv[1, g, near:]], axis=0
        ).T
        dk1 = jnp.zeros((near, HEAD_DIM), F32)
        dv1 = jnp.zeros((near, HEAD_DIM), F32)
        dk2 = jnp.zeros((HALF, HEAD_DIM), F32)
        dv2 = jnp.zeros((HALF, HEAD_DIM), F32)
        for pair in range(GROUP_HEADS // 2):
            first = g * GROUP_HEADS + 2 * pair
            qs = [head(q, h) for h in (first, first + 1)]
            ds = [head(do, h) for h in (first, first + 1)]
            fs = [f_in[h : h + 1, :] for h in (first, first + 1)]
            cs = [d_in[h : h + 1, :] for h in (first, first + 1)]
            w2 = p2[first // 2] * halves(*fs)
            s2 = (w2 * (dp2[first // 2] - halves(*cs))).astype(BF16)
            w2 = w2.astype(BF16)
            dk2 = dk2 + dot_nn(s2, second_half(*qs))
            dv2 = dv2 + dot_nn(w2, second_half(*ds))
            for i in range(2):
                h = first + i
                w1 = p1[h] * fs[i]
                s1 = (w1 * (dp1[h] - cs[i])).astype(BF16)
                w1 = w1.astype(BF16)
                dk1 = dk1 + dot_nn(s1, qs[i])
                dv1 = dv1 + dot_nn(w1, ds[i])
                half = slice(i * HALF, (i + 1) * HALF)
                ws = [w1, jnp.concatenate([w_in[h, 0], w_in[h, 1]], axis=1), jnp.concatenate([unseen, w2[:, half]], axis=1)]
                ss = [s1, jnp.concatenate([ds_in[h, 0], ds_in[h, 1]], axis=1), jnp.concatenate([unseen, s2[:, half]], axis=1)]
                o = dot_nn(v_t, jnp.concatenate(ws, axis=0))
                gq = dot_nn(k_t, jnp.concatenate(ss, axis=0))
                out[:, h * HEAD_DIM : (h + 1) * HEAD_DIM] = o.astype(BF16).T
                dq[:, h * HEAD_DIM : (h + 1) * HEAD_DIM] = (gq * SCALE).astype(BF16).T
        dk1 = dk1 * SCALE
        own[0, :, cols] = dk1[:SHARD].astype(BF16)
        own[1, :, cols] = dv1[:SHARD].astype(BF16)
        drk[:HALF, cols] = dk1[SHARD:].astype(BF16)
        drv[:HALF, cols] = dv1[SHARD:].astype(BF16)
        drk[HALF:, cols] = (dk2 * SCALE).astype(BF16)
        drv[HALF:, cols] = dv2.astype(BF16)
        wide = pl.ds(g * GROUP_HEADS * HEAD_DIM, GROUP_HEADS * HEAD_DIM)
        narrow = pl.ds(g * HEAD_DIM, HEAD_DIM)
        send(out, out_hbm, wide)
        send(dq, dq_hbm, wide)
        send(drk, drk_hbm, narrow)
        send(drv, drv_hbm, narrow)
    for copy in started:
        copy.wait()


def add_partials(a, b, c, d, keys, values):
    keys[...] = (
        (a[0].astype(F32) + b[0].astype(F32)) + (c[0].astype(F32) + d[0].astype(F32))
    ).astype(BF16)
    values[...] = (
        (a[1].astype(F32) + b[1].astype(F32)) + (c[1].astype(F32) + d[1].astype(F32))
    ).astype(BF16)


def in_vmem(x):
    return pltpu.with_memory_space_constraint(x, pltpu.VMEM)


def in_hbm(x):
    return pltpu.with_memory_space_constraint(x, pltpu.HBM)


def call(body, name, ins, outs, scratch=(), in_space=pltpu.VMEM, to_hbm=0, flops=0):
    return pl.pallas_call(
        body,
        name=name,
        in_specs=[pl.BlockSpec(memory_space=in_space)] * len(ins),
        out_specs=[pl.BlockSpec(memory_space=pltpu.HBM)] * to_hbm
        + [pl.BlockSpec(memory_space=pltpu.VMEM)] * (len(outs) - to_hbm),
        out_shape=outs,
        scratch_shapes=list(scratch),
        cost_estimate=pl.CostEstimate(flops=flops, bytes_accessed=1 << 20, transcendentals=0),
        compiler_params=pltpu.CompilerParams(vmem_limit_bytes=24 * 1024 * 1024),
    )(*ins)


def per_device(
    query, response_keys, response_values, prompt_keys, prompt_values, dout, row_slot, row_pos
):
    devices = lax.axis_size("rows")
    stride = devices // GROUP
    hbm = jax.ShapeDtypeStruct
    width = KV_HEADS * HEAD_DIM
    heads = (QUERY_HEADS, ROWS)
    stacked = jnp.stack([prompt_keys, prompt_values])

    def moved(block, steps):
        route = [(i, (i + steps * stride) % devices) for i in range(devices)]
        return lax.ppermute(block, "rows", route)

    remote = [moved(stacked, steps) for steps in STEPS]
    slot = row_slot.reshape(1, ROWS)
    pos = row_pos.reshape(1, ROWS)
    pair_heads = QUERY_HEADS // 2
    near = SHARD + HALF
    arrays = (
        query, dout, prompt_keys, prompt_values, response_keys, response_values, slot, pos
    )
    q, do, kv, p1, dp1, p2, dp2, m, l, c, live = map(
        in_vmem,
        call(
            local_forward,
            "local_forward",
            [in_hbm(x) for x in arrays],
            [
                VM((QUERY_HEADS, ROWS, HEAD_DIM), BF16),
                VM((QUERY_HEADS, ROWS, HEAD_DIM), BF16),
                VM((2, KV_HEADS, SHARD + ROWS, HEAD_DIM), BF16),
                VM((QUERY_HEADS, near, ROWS), F32),
                VM((QUERY_HEADS, near, ROWS), F32),
                VM((pair_heads, HALF, ROWS), F32),
                VM((pair_heads, HALF, ROWS), F32),
                VM(heads, F32),
                VM(heads, F32),
                VM(heads, F32),
                VM((1, ROWS), F32),
            ],
            [
                VM((ROWS, ROWS), F32),
                VM((1, ROWS), jnp.int32),
                VM((1, ROWS), jnp.int32),
                pltpu.SemaphoreType.DMA((10 + 2 * QUERY_HEADS,)),
            ],
            in_space=pltpu.HBM,
            flops=10**9,
        ),
    )
    partial = (2, SHARD, width)
    rx, ry, rz = remote
    early = (QUERY_HEADS, 2 * SHARD, ROWS)
    every = (QUERY_HEADS, ROWS // HALF, REMOTE, HALF)
    e, p, tx, ty, m2, l2, c2 = map(
        in_vmem,
        call(
            early_forward,
            "early_forward",
            [q, do, rx, ry, m, l, c],
            [VM(early, F32)] * 2 + [VM(heads, F32)] * 5,
            flops=10**9,
        ),
    )
    w, ds, f, d, *terms = call(
        late_pass,
        "late_pass",
        [q, do, rz, live, m, tx, ty, m2, l2, c2, e, p],
        [VM(every, BF16)] * 2 + [VM(heads, F32)] * 2 + [hbm(partial, BF16)] * 3,
        flops=10**9,
    )
    back = [moved(terms[n], -STEPS[n]) for n in SEND_ORDER]
    out, dq, drk, drv, own = call(
        local_backward,
        "local_backward",
        [q, do, kv, *remote, p1, dp1, p2, dp2] + [in_vmem(x) for x in (w, ds, f, d)],
        [
            hbm(query.shape, BF16),
            hbm(query.shape, BF16),
            hbm(response_keys.shape, BF16),
            hbm(response_keys.shape, BF16),
            hbm(partial, BF16),
        ],
        [
            VM(query.shape, BF16),
            VM(query.shape, BF16),
            VM(response_keys.shape, BF16),
            VM(response_keys.shape, BF16),
            pltpu.SemaphoreType.DMA((4 * KV_HEADS,)),
        ],
        to_hbm=4,
        flops=10**6,
    )
    gpk, gpv = call(
        add_partials,
        "add_partials",
        [own, *back],
        [hbm(prompt_keys.shape, BF16), hbm(prompt_keys.shape, BF16)],
    )
    return out, dq, drk, drv, gpk, gpv


def solution(mesh):
    rows = P("rows", None)
    return jax.shard_map(
        per_device,
        mesh=mesh,
        in_specs=(rows,) * 6 + (P("rows"),) * 2,
        out_specs=(rows,) * 6,
        check_vma=False,
    )
```

```python
import jax
import jax.numpy as jnp
from jax import lax
from jax.experimental import pallas as pl
from jax.experimental.pallas import tpu as pltpu
from jax.sharding import PartitionSpec as P

QUERY_HEADS = 16
KV_HEADS = 2
GROUP_HEADS = QUERY_HEADS // KV_HEADS
HEAD_DIM = 128
GROUP = 4
STEPS = (3, 1, 2)
SEND_ORDER = (0, 1, 2)
ROWS = 256
HALF = 128
SHARD = 128
REMOTE = (GROUP - 1) * SHARD
SCALE = HEAD_DIM**-0.5
EXP2_SCALE = SCALE * 1.4426950408889634
NEG = -1e30
LOAD_AT = (0, 6)
LATE_SKEW = 2
F32 = jnp.float32
BF16 = jnp.bfloat16
VM = pltpu.VMEM


def dot_nt(a, b):
    return lax.dot_general(a, b, (((1,), (1,)), ((), ())), preferred_element_type=F32)


def dot_nn(a, b):
    return lax.dot_general(a, b, (((1,), (0,)), ((), ())), preferred_element_type=F32)


def col_max(x):
    return jnp.max(x, axis=0, keepdims=True)


def col_sum(x):
    return jnp.sum(x, axis=0, keepdims=True)


def second_half(a, b):
    return jnp.concatenate([a[HALF:], b[HALF:]], axis=0)


def halves(a, b):
    return jnp.concatenate([a[:, HALF:], b[:, HALF:]], axis=1)


def unhalves(x, which, fill):
    return jnp.concatenate([fill, x[:, which * HALF : (which + 1) * HALF]], axis=1)


def local_forward(
    q_in, do_in, pk, pv, rk, rv, slot_in, pos_in,
    q, do, kv, p1, dp1, p2, dp2, m_out, l_out, c_out, live,
    bias, slot, pos, sems,
):
    pieces = [
        (slot_in, slot),
        (pos_in, pos),
    ]
    for g in range(KV_HEADS):
        cols = pl.ds(g * HEAD_DIM, HEAD_DIM)
        for n, (shard, rows) in enumerate(((pk, rk), (pv, rv))):
            pieces.append((shard.at[:, cols], kv.at[n, g, pl.ds(0, SHARD)]))
            pieces.append((rows.at[:, cols], kv.at[n, g, pl.ds(SHARD, ROWS)]))
    for h in range(QUERY_HEADS):
        span = pl.ds(h * HEAD_DIM, HEAD_DIM)
        pieces.append((q_in.at[:, span], q.at[h]))
        pieces.append((do_in.at[:, span], do.at[h]))
    copies = [pltpu.make_async_copy(a, b, sems.at[n]) for n, (a, b) in enumerate(pieces)]
    for copy in copies:
        copy.start()
    copies[0].wait()
    copies[1].wait()
    slot_row = jnp.broadcast_to(slot[...], (ROWS, ROWS)).astype(F32)
    pos_row = jnp.broadcast_to(pos[...], (ROWS, ROWS)).astype(F32)
    slot_col = slot_row.T
    pos_col = pos_row.T
    seen = (slot_col == slot_row) & (slot_col >= 0) & (pos_col <= pos_row)
    bias[...] = jnp.where(seen, 0.0, NEG)
    live[...] = (slot[...] >= 0).astype(F32)
    nothing = jnp.full((1, HALF), NEG, F32)
    zero = jnp.zeros((1, HALF), F32)
    near = SHARD + HALF
    for copy in copies[2:10]:
        copy.wait()
    for g in range(KV_HEADS):
        cols = slice(g * HEAD_DIM, (g + 1) * HEAD_DIM)
        k1 = kv[0, g, :near]
        v1 = kv[1, g, :near]
        k2 = kv[0, g, near:]
        v2 = kv[1, g, near:]
        for pair in range(GROUP_HEADS // 2):
            first = g * GROUP_HEADS + 2 * pair
            if first in LOAD_AT:
                stop = min([n for n in LOAD_AT if n > first] + [QUERY_HEADS])
                for copy in copies[10 + 2 * first : 10 + 2 * stop]:
                    copy.wait()
            qs = [head(q, h) for h in (first, first + 1)]
            ds = [head(do, h) for h in (first, first + 1)]
            b2 = bias[HALF:, HALF:]
            s2 = dot_nt(k2, second_half(*qs)) + jnp.concatenate([b2, b2], axis=1)
            m2 = col_max(s2)
            ms, ls, cs = [], [], []
            for i in range(2):
                s1 = dot_nt(k1, qs[i])
                s1 = jnp.concatenate([s1[:SHARD], s1[SHARD:] + bias[:HALF, :]], axis=0)
                m = jnp.maximum(col_max(s1), unhalves(m2, i, nothing))
                e1 = jnp.exp2((s1 - m) * EXP2_SCALE)
                g1 = dot_nt(v1, ds[i])
                p1[first + i] = e1
                dp1[first + i] = g1
                ms.append(m)
                ls.append(col_sum(e1))
                cs.append(col_sum(e1 * g1))
            e2 = jnp.exp2((s2 - halves(*ms)) * EXP2_SCALE)
            g2 = dot_nt(v2, second_half(*ds))
            p2[first // 2] = e2
            dp2[first // 2] = g2
            l2 = col_sum(e2)
            c2 = col_sum(e2 * g2)
            for i in range(2):
                h = first + i
                m_out[h : h + 1, :] = ms[i]
                l_out[h : h + 1, :] = ls[i] + unhalves(l2, i, zero)
                c_out[h : h + 1, :] = cs[i] + unhalves(c2, i, zero)


def head(ref, h):
    return ref[h]


def columns_of(h):
    g = h // GROUP_HEADS
    return slice(g * HEAD_DIM, (g + 1) * HEAD_DIM)


def block(n):
    return slice(n * SHARD, (n + 1) * SHARD)


def early_forward(q, do, rx, ry, m_in, l_in, c_in, e_out, p_out, tx, ty, m_out, l_out, c_out):
    for h in range(QUERY_HEADS):
        cols = columns_of(h)
        row = slice(h, h + 1)
        s = dot_nt(jnp.concatenate([rx[0, :, cols], ry[0, :, cols]], axis=0), head(q, h))
        pressure = dot_nt(jnp.concatenate([rx[1, :, cols], ry[1, :, cols]], axis=0), head(do, h))
        m_old = m_in[row, :]
        m = m_old
        tops, sums, centres = [], [], []
        for n in range(2):
            top = col_max(s[block(n)])
            e = jnp.exp2((s[block(n)] - top) * EXP2_SCALE)
            p = pressure[block(n)]
            e_out[h, block(n)] = e
            p_out[h, block(n)] = p
            tops.append(top)
            sums.append(col_sum(e))
            centres.append(col_sum(e * p))
            m = jnp.maximum(m, top)
        back = jnp.exp2((m_old - m) * EXP2_SCALE)
        total = l_in[row, :] * back
        centre = c_in[row, :] * back
        for top, a, b in zip(tops, sums, centres):
            factor = jnp.exp2((top - m) * EXP2_SCALE)
            total = total + a * factor
            centre = centre + b * factor
        tx[row, :] = tops[0]
        ty[row, :] = tops[1]
        m_out[row, :] = m
        l_out[row, :] = total
        c_out[row, :] = centre


def late_pass(
    q, do, rz, live, m_first, tx, ty, m_in, l_in, c_in, e_in, p_in,
    w_out, ds_out, f_out, d_out, gx, gy, gz,
):
    alive = live[...]

    def slopes_of(h):
        cols = columns_of(h)
        row = slice(h, h + 1)
        s = dot_nt(rz[0, :, cols], head(q, h))
        pressure = dot_nt(rz[1, :, cols], head(do, h))
        m_old = m_in[row, :]
        top = col_max(s)
        e = jnp.exp2((s - top) * EXP2_SCALE)
        m = jnp.maximum(m_old, top)
        back = jnp.exp2((m_old - m) * EXP2_SCALE)
        factor = jnp.exp2((top - m) * EXP2_SCALE)
        total = l_in[row, :] * back + col_sum(e) * factor
        inv = 1.0 / total
        centre = (c_in[row, :] * back + col_sum(e * pressure) * factor) * inv
        inv = inv * alive
        f_out[row, :] = jnp.exp2((m_first[row, :] - m) * EXP2_SCALE) * inv
        d_out[row, :] = centre
        lows, slopes = [], []
        for n, (a, b) in enumerate(
            ((e_in[h, block(0)], p_in[h, block(0)]), (e_in[h, block(1)], p_in[h, block(1)]), (e, pressure))
        ):
            if n < 2:
                factor = jnp.exp2(((tx, ty)[n][row, :] - m) * EXP2_SCALE)
            else:
                factor = jnp.exp2((top - m) * EXP2_SCALE)
            w = a * (factor * inv)
            lows.append(w.astype(BF16))
            slopes.append((w * (b - centre)).astype(BF16))
            for half in range(2):
                w_out[h, half, block(n)] = lows[-1][:, half * HALF : (half + 1) * HALF]
                ds_out[h, half, block(n)] = slopes[-1][:, half * HALF : (half + 1) * HALF]
        return jnp.concatenate(lows, axis=0), jnp.concatenate(slopes, axis=0)

    def store(cols, dk, dv):
        for n, out in enumerate((gx, gy, gz)):
            out[0, :, cols] = (dk[block(n)] * SCALE).astype(BF16)
            out[1, :, cols] = dv[block(n)].astype(BF16)

    skewed_terms(q, do, slopes_of, store, LATE_SKEW)


def skewed_terms(q, do, slopes_of, store, skew):
    made = {}
    dk = dv = None
    for t in range(QUERY_HEADS + skew):
        if t < QUERY_HEADS:
            made[t] = slopes_of(t)
        h = t - skew
        if h < 0:
            continue
        low, slopes = made.pop(h)
        k = dot_nn(slopes, head(q, h))
        v = dot_nn(low, head(do, h))
        first = h % GROUP_HEADS == 0
        dk = k if first else dk + k
        dv = v if first else dv + v
        if h % GROUP_HEADS == GROUP_HEADS - 1:
            store(columns_of(h), dk, dv)


def local_backward(
    q, do, kv, rx, ry, rz, p1, dp1, p2, dp2, w_in, ds_in, f_in, d_in,
    out_hbm, dq_hbm, drk_hbm, drv_hbm, own,
    out, dq, drk, drv, sems,
):
    started = []

    def send(buffer, target, cols):
        copy = pltpu.make_async_copy(buffer.at[:, cols], target.at[:, cols], sems.at[len(started)])
        copy.start()
        started.append(copy)

    near = SHARD + HALF
    unseen = jnp.zeros((HALF, HALF), BF16)
    for g in range(KV_HEADS):
        cols = slice(g * HEAD_DIM, (g + 1) * HEAD_DIM)
        shards = (rx, ry, rz)
        k_t = jnp.concatenate(
            [kv[0, g, :near]] + [r[0, :, cols] for r in shards] + [kv[0, g, near:]], axis=0
        ).T
        v_t = jnp.concatenate(
            [kv[1, g, :near]] + [r[1, :, cols] for r in shards] + [kv[1, g, near:]], axis=0
        ).T
        dk1 = jnp.zeros((near, HEAD_DIM), F32)
        dv1 = jnp.zeros((near, HEAD_DIM), F32)
        dk2 = jnp.zeros((HALF, HEAD_DIM), F32)
        dv2 = jnp.zeros((HALF, HEAD_DIM), F32)
        for pair in range(GROUP_HEADS // 2):
            first = g * GROUP_HEADS + 2 * pair
            qs = [head(q, h) for h in (first, first + 1)]
            ds = [head(do, h) for h in (first, first + 1)]
            fs = [f_in[h : h + 1, :] for h in (first, first + 1)]
            cs = [d_in[h : h + 1, :] for h in (first, first + 1)]
            w2 = p2[first // 2] * halves(*fs)
            s2 = (w2 * (dp2[first // 2] - halves(*cs))).astype(BF16)
            w2 = w2.astype(BF16)
            dk2 = dk2 + dot_nn(s2, second_half(*qs))
            dv2 = dv2 + dot_nn(w2, second_half(*ds))
            for i in range(2):
                h = first + i
                w1 = p1[h] * fs[i]
                s1 = (w1 * (dp1[h] - cs[i])).astype(BF16)
                w1 = w1.astype(BF16)
                dk1 = dk1 + dot_nn(s1, qs[i])
                dv1 = dv1 + dot_nn(w1, ds[i])
                half = slice(i * HALF, (i + 1) * HALF)
                ws = [w1, jnp.concatenate([w_in[h, 0], w_in[h, 1]], axis=1), jnp.concatenate([unseen, w2[:, half]], axis=1)]
                ss = [s1, jnp.concatenate([ds_in[h, 0], ds_in[h, 1]], axis=1), jnp.concatenate([unseen, s2[:, half]], axis=1)]
                o = dot_nn(v_t, jnp.concatenate(ws, axis=0))
                gq = dot_nn(k_t, jnp.concatenate(ss, axis=0))
                out[:, h * HEAD_DIM : (h + 1) * HEAD_DIM] = o.astype(BF16).T
                dq[:, h * HEAD_DIM : (h + 1) * HEAD_DIM] = (gq * SCALE).astype(BF16).T
        dk1 = dk1 * SCALE
        own[0, :, cols] = dk1[:SHARD].astype(BF16)
        own[1, :, cols] = dv1[:SHARD].astype(BF16)
        drk[:HALF, cols] = dk1[SHARD:].astype(BF16)
        drv[:HALF, cols] = dv1[SHARD:].astype(BF16)
        drk[HALF:, cols] = (dk2 * SCALE).astype(BF16)
        drv[HALF:, cols] = dv2.astype(BF16)
        wide = pl.ds(g * GROUP_HEADS * HEAD_DIM, GROUP_HEADS * HEAD_DIM)
        narrow = pl.ds(g * HEAD_DIM, HEAD_DIM)
        send(out, out_hbm, wide)
        send(dq, dq_hbm, wide)
        send(drk, drk_hbm, narrow)
        send(drv, drv_hbm, narrow)
    for copy in started:
        copy.wait()


def add_partials(a, b, c, d, keys, values):
    keys[...] = (
        (a[0].astype(F32) + b[0].astype(F32)) + (c[0].astype(F32) + d[0].astype(F32))
    ).astype(BF16)
    values[...] = (
        (a[1].astype(F32) + b[1].astype(F32)) + (c[1].astype(F32) + d[1].astype(F32))
    ).astype(BF16)


def in_vmem(x):
    return pltpu.with_memory_space_constraint(x, pltpu.VMEM)


def in_hbm(x):
    return pltpu.with_memory_space_constraint(x, pltpu.HBM)


def call(body, name, ins, outs, scratch=(), in_space=pltpu.VMEM, to_hbm=0, flops=0):
    return pl.pallas_call(
        body,
        name=name,
        in_specs=[pl.BlockSpec(memory_space=in_space)] * len(ins),
        out_specs=[pl.BlockSpec(memory_space=pltpu.HBM)] * to_hbm
        + [pl.BlockSpec(memory_space=pltpu.VMEM)] * (len(outs) - to_hbm),
        out_shape=outs,
        scratch_shapes=list(scratch),
        cost_estimate=pl.CostEstimate(flops=flops, bytes_accessed=1 << 20, transcendentals=0),
        compiler_params=pltpu.CompilerParams(vmem_limit_bytes=24 * 1024 * 1024),
    )(*ins)


def per_device(
    query, response_keys, response_values, prompt_keys, prompt_values, dout, row_slot, row_pos
):
    devices = lax.axis_size("rows")
    stride = devices // GROUP
    hbm = jax.ShapeDtypeStruct
    width = KV_HEADS * HEAD_DIM
    heads = (QUERY_HEADS, ROWS)
    stacked = jnp.stack([prompt_keys, prompt_values])

    def moved(block, steps):
        route = [(i, (i + steps * stride) % devices) for i in range(devices)]
        return lax.ppermute(block, "rows", route)

    remote = [moved(stacked, steps) for steps in STEPS]
    slot = row_slot.reshape(1, ROWS)
    pos = row_pos.reshape(1, ROWS)
    pair_heads = QUERY_HEADS // 2
    near = SHARD + HALF
    arrays = (
        query, dout, prompt_keys, prompt_values, response_keys, response_values, slot, pos
    )
    q, do, kv, p1, dp1, p2, dp2, m, l, c, live = map(
        in_vmem,
        call(
            local_forward,
            "local_forward",
            [in_hbm(x) for x in arrays],
            [
                VM((QUERY_HEADS, ROWS, HEAD_DIM), BF16),
                VM((QUERY_HEADS, ROWS, HEAD_DIM), BF16),
                VM((2, KV_HEADS, SHARD + ROWS, HEAD_DIM), BF16),
                VM((QUERY_HEADS, near, ROWS), F32),
                VM((QUERY_HEADS, near, ROWS), F32),
                VM((pair_heads, HALF, ROWS), F32),
                VM((pair_heads, HALF, ROWS), F32),
                VM(heads, F32),
                VM(heads, F32),
                VM(heads, F32),
                VM((1, ROWS), F32),
            ],
            [
                VM((ROWS, ROWS), F32),
                VM((1, ROWS), jnp.int32),
                VM((1, ROWS), jnp.int32),
                pltpu.SemaphoreType.DMA((10 + 2 * QUERY_HEADS,)),
            ],
            in_space=pltpu.HBM,
            flops=10**9,
        ),
    )
    partial = (2, SHARD, width)
    rx, ry, rz = remote
    early = (QUERY_HEADS, 2 * SHARD, ROWS)
    every = (QUERY_HEADS, ROWS // HALF, REMOTE, HALF)
    e, p, tx, ty, m2, l2, c2 = map(
        in_vmem,
        call(
            early_forward,
            "early_forward",
            [q, do, rx, ry, m, l, c],
            [VM(early, F32)] * 2 + [VM(heads, F32)] * 5,
            flops=10**9,
        ),
    )
    w, ds, f, d, *terms = call(
        late_pass,
        "late_pass",
        [q, do, rz, live, m, tx, ty, m2, l2, c2, e, p],
        [VM(every, BF16)] * 2 + [VM(heads, F32)] * 2 + [hbm(partial, BF16)] * 3,
        flops=10**9,
    )
    back = [moved(terms[n], -STEPS[n]) for n in SEND_ORDER]
    out, dq, drk, drv, own = call(
        local_backward,
        "local_backward",
        [q, do, kv, *remote, p1, dp1, p2, dp2] + [in_vmem(x) for x in (w, ds, f, d)],
        [
            hbm(query.shape, BF16),
            hbm(query.shape, BF16),
            hbm(response_keys.shape, BF16),
            hbm(response_keys.shape, BF16),
            hbm(partial, BF16),
        ],
        [
            VM(query.shape, BF16),
            VM(query.shape, BF16),
            VM(response_keys.shape, BF16),
            VM(response_keys.shape, BF16),
            pltpu.SemaphoreType.DMA((4 * KV_HEADS,)),
        ],
        to_hbm=4,
        flops=10**6,
    )
    gpk, gpv = call(
        add_partials,
        "add_partials",
        [own, *back],
        [hbm(prompt_keys.shape, BF16), hbm(prompt_keys.shape, BF16)],
    )
    return out, dq, drk, drv, gpk, gpv


def solution(mesh):
    rows = P("rows", None)
    return jax.shard_map(
        per_device,
        mesh=mesh,
        in_specs=(rows,) * 6 + (P("rows"),) * 2,
        out_specs=(rows,) * 6,
        check_vma=False,
    )
```
